128 devices in a mesh: dp: 8 (over z, y_lo), space: 16 (over y_hi, x, core).
Axes of the slice: x: 4, y: 4 (y_hi: 2, y_lo: 2; y = y_hi * 2 + y_lo), z: 4, core: 2. Of those that a mesh axis runs over, the one named last changes fastest.
Arguments:
- activation: bfloat16 [8, 16, 64, 128, 128], P('dp', None, 'space'), may hold values from -6 to 6
- cotangent: bfloat16 [8, 16, 64, 128, 128], P('dp', None, 'space'), may hold values from -6 to 6
- volume: bfloat16 [8, 1, 64, 128, 128], P('dp', None, 'space'), may hold values from -6 to 6
- dec_weight: bfloat16 [27, 16, 16], replicated, may hold values from -0.3125 to 0.3125
- enc_grad: float32 [8, 16, 7376], P('dp', 'space'), may hold values from -6 to 6
- params: float32 [14288], P('dp'), may hold values from -0.6 to 0.6
- moment: float32 [14288], P('dp'), may hold values from -0.3 to 0.3
- second: float32 [14288], P('dp'), may hold values from 0.001 to 0.004
Outputs:
- grad_input: bfloat16 [8, 16, 64, 128, 128], P('dp', None, 'space')
- new_params: float32 [14288], P('dp')
- new_moment: float32 [14288], P('dp')
- new_second: float32 [14288], P('dp')
- working: bfloat16 [14288], replicated
- encoded: bfloat16 [8, 16, 64, 128, 128], P('dp', None, 'space')
The draws below stay inside these ranges and needn't reach their ends.
All inputs are finite; a program needn't handle non-finite values.
Results may differ from the reference program's by a relative error of at most 0.0073.
Values may be sent and summed in bfloat16 or wider, within the bound.
No kernel may reach another device: no remote copies, remote signals or barrier semaphores. Data moves between devices by JAX's collectives and lax.ppermute only.
A program may use at most 256 MiB of HBM per device.

```python
import math
import jax
import jax.numpy as jnp
from jax import lax

C = 16
H = 128
W = 128
BATCH = 8
DEPTH = 64
VOXELS = 8388608
ENC_PARAMS = 7376
PARAMS = 14288
N_DP = 8
N_SPACE = 16


def steps_of(rng, dims, shards, smallest, top_value):
    gain, own = 1.0, jax.random.fold_in(rng, 6)
    for position, shards_of in shards:
        heights = jnp.exp(jax.random.uniform(jax.random.fold_in(own, position), (shards_of,), jnp.float32, smallest / len(shards), top_value / len(shards)))
        gain = gain * jnp.repeat(heights, dims[position] // shards_of).reshape([-1 if axis == position else 1 for axis in range(len(dims))])
    return gain


def centred(rng, dims, scale, most, cuts=(), dtype=jnp.bfloat16):
    result = scale * jax.random.normal(rng, dims, jnp.float32)
    if cuts:
        result = result * steps_of(rng, dims, cuts, -0.22, 0.18)
    return jnp.clip(result, -most, most).astype(dtype)


def setup_inputs(seed: int = 0) -> dict:
    seeds = jax.random.split(jax.random.key(seed), 9)
    activation = centred(seeds[0], (BATCH, C, DEPTH, H, W), 1.0, 6.0, ((0, 8), (2, 16)))
    cotangent = centred(seeds[1], (BATCH, C, DEPTH, H, W), 1.0, 6.0, ((0, 8), (2, 16)))
    volume = centred(seeds[2], (BATCH, 1, DEPTH, H, W), 1.0, 6.0, ((0, 8), (2, 16)))
    dec_weight = centred(seeds[3], (27, C, C), (27 * C) ** -0.5, 0.3125)
    enc_grad = centred(seeds[4], (N_DP, N_SPACE, ENC_PARAMS), 1.0, 6.0, ((0, 8), (1, 16)), jnp.float32)
    params = centred(seeds[5], (PARAMS,), 0.1, 0.6, ((0, 8),), jnp.float32)
    moment = centred(seeds[6], (PARAMS,), 0.05, 0.3, ((0, 8),), jnp.float32)
    second = jnp.clip(jnp.exp(math.log(0.004) - 1.3862944 * jax.random.uniform(seeds[7], (PARAMS,), jnp.float32) ** steps_of(seeds[7], (PARAMS,), ((0, 8),), -0.2, 0.2)), 0.001, 0.004)
    return {"activation": activation, "cotangent": cotangent, "volume": volume, "dec_weight": dec_weight, "enc_grad": enc_grad, "params": params, "moment": moment, "second": second}


def lateral_stack(padded_in):
    height = padded_in.shape[2]
    columns = padded_in.shape[3]
    spread = jnp.pad(padded_in, ((0, 0), (0, 0), (1, 1), (1, 1)))
    return jnp.concatenate([spread[:, :, row_off:row_off + height, col_off:col_off + columns] for row_off in range(3) for col_off in range(3)], axis=0)

def convolve(padded_in, weight):
    stacked = lateral_stack(padded_in).astype(jnp.float32)
    planes = padded_in.shape[1] - 2
    kernels = weight.astype(jnp.float32).reshape(3, 9 * weight.shape[1], weight.shape[2])
    summed = jnp.zeros((weight.shape[2], planes, padded_in.shape[2], padded_in.shape[3]), jnp.float32)
    for depth_off in range(3):
        summed = summed + jnp.einsum('ko,kdhw->odhw', kernels[depth_off], stacked[:, depth_off:depth_off + planes])
    return summed

def correlate(padded_in, cotan):
    stacked = lateral_stack(padded_in).astype(jnp.float32)
    planes = padded_in.shape[1] - 2
    pieces = [jnp.einsum('kdhw,odhw->ko', stacked[:, depth_off:depth_off + planes], cotan.astype(jnp.float32)) for depth_off in range(3)]
    return jnp.stack(pieces).reshape(27, padded_in.shape[0], cotan.shape[0])

def depth_pad(field):
    return jnp.pad(field, ((0, 0), (1, 1), (0, 0), (0, 0)))

def reference(activation, cotangent, volume, dec_weight, enc_grad, params, moment, second):
    flipped = dec_weight[::-1].transpose(0, 2, 1)

    def per_crop(item):
        act_crop, cot_crop = item
        weight_grad = correlate(depth_pad(act_crop), cot_crop)
        grad_crop = convolve(depth_pad(cot_crop), flipped).astype(jnp.bfloat16)
        return (weight_grad, grad_crop)
    weight_grads, grad_input = lax.map(per_crop, (activation, cotangent))
    dec_grad = lax.optimization_barrier(jnp.sum(weight_grads, axis=0)) / math.sqrt(VOXELS)
    enc_sum = lax.optimization_barrier(jnp.sum(enc_grad, axis=(0, 1))) / math.sqrt(N_DP * N_SPACE)
    gradient = jnp.concatenate([dec_grad.reshape(-1), enc_sum])
    new_moment = 0.9 * moment + 0.1 * gradient
    new_second = 0.999 * second + 0.001 * gradient * gradient
    new_params = params - 0.01 * new_moment / (jnp.sqrt(new_second) + 1e-08)
    working = new_params.astype(jnp.bfloat16)
    offset = 27 * C * C
    weight_one = working[offset:offset + 27 * C].reshape(27, 1, C)
    offset = offset + 27 * C
    bias_one = working[offset:offset + C].astype(jnp.float32)
    offset = offset + C
    weight_two = working[offset:offset + 27 * C * C].reshape(27, C, C)
    offset = offset + 27 * C * C
    bias_two = working[offset:offset + C].astype(jnp.float32)

    def forward(crop):
        first = jax.nn.relu(convolve(depth_pad(crop), weight_one) + bias_one[:, None, None, None]).astype(jnp.bfloat16)
        return jax.nn.relu(convolve(depth_pad(first), weight_two) + bias_two[:, None, None, None]).astype(jnp.bfloat16)
    encoded = lax.map(forward, volume)
    return (grad_input, new_params, new_moment, new_second, working, encoded)
```

```python
import math

import jax
import jax.numpy as jnp
import numpy as np
from jax import lax
from jax.experimental import pallas as pl
from jax.experimental.pallas import tpu as pltpu
from jax.sharding import PartitionSpec as P

BF = jnp.bfloat16
F32 = jnp.float32
VMEM = pltpu.VMEM
LIMIT = 48 * 1024 * 1024


def exchange_matrix():
    rows = lax.broadcasted_iota(jnp.int32, (256, 256), 0)
    cols = lax.broadcasted_iota(jnp.int32, (256, 256), 1)
    return jnp.where(cols == (rows % 16) * 16 + rows // 16, 1.0, 0.0).astype(BF)


def mm(left, right):
    return lax.dot_general(left, right, (((1,), (0,)), ((), ())), preferred_element_type=F32)


def mm_lanes(left, right):
    return lax.dot_general(left, right, (((1,), (1,)), ((), ())), preferred_element_type=F32)


def lane_masks(rows):
    lanes = lax.broadcasted_iota(jnp.int32, (rows, 128), 1)
    return lanes != 0, lanes != 127


def from_left(value, keep):
    return jnp.where(keep, pltpu.roll(value, 1, 1), 0.0)


def from_right(value, keep):
    return jnp.where(keep, pltpu.roll(value, 127, 1), 0.0)


def rows_first(act_ref, cot_ref, act_out, cot_out):
    step = pl.program_id(0)
    swap = exchange_matrix()
    not_first, not_last = lane_masks(256)

    @pl.when(step == 0)
    def _():
        edge = jnp.zeros((4, 1, 16, 128), BF)
        cot_out[:, 0:1] = edge
        cot_out[:, 129:130] = edge

    for pair in range(2):
        cells = jnp.concatenate(
            [cot_ref[:, 2 * pair + z].reshape(256, 128) for z in range(2)], axis=1
        )
        moved = mm(swap, cells)
        for z in range(2):
            part = moved[:, z * 128 : (z + 1) * 128].astype(BF).reshape(16, 16, 128)
            cot_out[2 * pair + z, pl.ds(step * 16 + 1, 16)] = part
        cells = jnp.concatenate(
            [act_ref[:, 2 * pair + z].reshape(256, 128) for z in range(2)], axis=1
        )
        moved = mm(swap, cells)
        for z in range(2):
            part = moved[:, z * 128 : (z + 1) * 128]
            shifted = (from_left(part, not_first), part, from_right(part, not_last))
            for dx in range(3):
                act_out[dx, 2 * pair + z] = shifted[dx].astype(BF).reshape(16, 16, 128)


def call_rows_first(act, cot):
    block = pl.BlockSpec((16, 4, 16, 128), lambda j: (0, 0, j, 0))
    return pl.pallas_call(
        rows_first,
        grid=(8,),
        in_specs=[block, block],
        out_specs=[
            pl.BlockSpec((3, 4, 16, 16, 128), lambda j: (0, 0, j, 0, 0)),
            pl.BlockSpec((4, 130, 16, 128), lambda j: (0, 0, 0, 0)),
        ],
        out_shape=[
            jax.ShapeDtypeStruct((3, 4, 128, 16, 128), BF),
            jax.ShapeDtypeStruct((4, 130, 16, 128), BF),
        ],
        compiler_params=pltpu.CompilerParams(vmem_limit_bytes=LIMIT),
        name="rows_first",
    )(act, cot)


def window(planes, base):
    return jnp.concatenate(
        [ref[z, pl.ds(base, 4)].reshape(64, 128) for ref, z in planes], axis=0
    )


def weight_sum(odd_ref, near_ref, far_ref, act_ref, cot_ref, grad_ref, rim_ref, total):
    step = pl.program_id(0)
    odd = odd_ref[0]
    swap = exchange_matrix()

    @pl.when(step == 0)
    def _():
        total[...] = jnp.zeros_like(total)
        edge = jnp.zeros((2, 1, 16, 128), BF)
        rim_ref[:, 0:1] = edge
        rim_ref[:, 129:130] = edge

        def body(j, carry):
            rows = pl.ds(pl.multiple_of(j * 16, 16), 16)
            cells = jnp.concatenate(
                [ref[0:16, rows].reshape(256, 128) for ref in (near_ref, far_ref)], axis=1
            )
            moved = mm(swap, cells).astype(BF)
            here = pl.ds(j * 16 + 1, 16)
            rim_ref[1 - odd, here] = moved[:, :128].reshape(16, 16, 128)
            rim_ref[odd, here] = moved[:, 128:].reshape(16, 16, 128)
            return carry

        lax.fori_loop(0, 8, body, 0)

    planes = [(rim_ref, 0)] + [(cot_ref, z) for z in range(4)] + [(rim_ref, 1)]
    left, right = [], []
    for q in range(8):
        base = step * 16 + 2 * q
        for zt in range(2):
            left.append(
                jnp.concatenate(
                    [
                        act_ref[dx, 2 * zt + z, 2 * q : 2 * q + 2].reshape(32, 128)
                        for dx in range(3)
                        for z in range(2)
                    ],
                    axis=0,
                )
            )
            right.append(window(planes[2 * zt : 2 * zt + 4], base))
    total[...] += mm_lanes(jnp.concatenate(left, axis=1), jnp.concatenate(right, axis=1))

    @pl.when(step == 7)
    def _():
        for dx in range(3):
            summed = None
            for z in range(2):
                for r in range(2):
                    start = ((dx * 2 + z) * 2 + r) * 16
                    part = total[start : start + 16]
                    shift = (z * 4 + r) * 16
                    if shift:
                        part = pltpu.roll(part, 256 - shift, 1)
                    summed = part if summed is None else summed + part
            grad_ref[dx * 16 : (dx + 1) * 16] = summed


def call_weight_sum(odd, near, far, act_rows, cot_rows):
    whole = lambda shape: pl.BlockSpec(shape, lambda j: (0,) * len(shape))
    return pl.pallas_call(
        weight_sum,
        grid=(8,),
        in_specs=[
            pl.BlockSpec(memory_space=pltpu.SMEM),
            whole((18, 128, 128)),
            whole((18, 128, 128)),
            pl.BlockSpec((3, 4, 16, 16, 128), lambda j: (0, 0, j, 0, 0)),
            whole((4, 130, 16, 128)),
        ],
        out_specs=[whole((48, 256)), whole((2, 130, 16, 128))],
        out_shape=[
            jax.ShapeDtypeStruct((48, 256), F32),
            jax.ShapeDtypeStruct((2, 130, 16, 128), BF),
        ],
        scratch_shapes=[pltpu.VMEM((192, 256), F32)],
        compiler_params=pltpu.CompilerParams(vmem_limit_bytes=LIMIT),
        name="weight_sum",
    )(odd, near, far, act_rows, cot_rows)


def conv_block(step, planes, kernel, out_ref, held, finish):
    swap = exchange_matrix()
    not_first, not_last = lane_masks(64)
    for q in range(8):
        base = step * 16 + 2 * q
        cells = jnp.concatenate(
            [window(planes[2 * zt : 2 * zt + 4], base) for zt in range(2)], axis=1
        )
        product = mm(kernel, cells)
        for zt in range(2):
            part = product[:, zt * 128 : (zt + 1) * 128]
            summed = (
                part[64:128]
                + from_left(part[0:64], not_first)
                + from_right(part[128:192], not_last)
            )
            rounded = finish(summed).astype(BF).reshape(2, 2, 16, 128)
            for z in range(2):
                held[2 * zt + z, 2 * q : 2 * q + 2] = rounded[z]
    for zt in range(2):
        cells = jnp.concatenate(
            [held[2 * zt + z].reshape(256, 128) for z in range(2)], axis=1
        )
        moved = mm(swap, cells).astype(BF)
        for z in range(2):
            out_ref[:, 2 * zt + z] = moved[:, z * 128 : (z + 1) * 128].reshape(16, 16, 128)


def shifted_kernels(bases):
    return jnp.concatenate(
        [
            pltpu.roll(base, (z * 4 + r) * 16, 1) if z + r else base
            for base in bases
            for z in range(2)
            for r in range(2)
        ],
        axis=0,
    ).astype(BF)


def input_grad(weight_ref, cot_ref, rim_ref, out_ref, kernel, held):
    step = pl.program_id(0)

    @pl.when(step == 0)
    def _():
        bases = []
        for dx in range(3):
            base = jnp.zeros((16, 256), F32)
            for dz in range(3):
                for dy in range(3):
                    tap = weight_ref[26 - (9 * dz + 3 * dy + dx)].astype(F32)
                    tap = jnp.concatenate([tap, jnp.zeros((16, 240), F32)], axis=1)
                    place = (dz * 4 + dy) * 16
                    base = base + (pltpu.roll(tap, place, 1) if place else tap)
            bases.append(base)
        kernel[...] = shifted_kernels(bases)

    planes = [(rim_ref, 0)] + [(cot_ref, z) for z in range(4)] + [(rim_ref, 1)]
    conv_block(step, planes, kernel[...], out_ref, held, lambda value: value)


def call_input_grad(weight, cot_rows, rim_rows):
    whole = lambda shape: pl.BlockSpec(shape, lambda j: (0,) * len(shape))
    return pl.pallas_call(
        input_grad,
        grid=(8,),
        in_specs=[whole((27, 16, 16)), whole((4, 130, 16, 128)), whole((2, 130, 16, 128))],
        out_specs=pl.BlockSpec((16, 4, 16, 128), lambda j: (0, 0, j, 0)),
        out_shape=jax.ShapeDtypeStruct((16, 4, 128, 128), BF),
        scratch_shapes=[pltpu.VMEM((192, 256), BF), pltpu.VMEM((4, 16, 16, 128), BF)],
        compiler_params=pltpu.CompilerParams(vmem_limit_bytes=LIMIT),
        name="input_grad",
    )(weight, cot_rows, rim_rows)


def placement():
    table = np.zeros((8, 64, 1408), np.float32)

    def put(group, column):
        table[group % 8, group // 8, column] = 1.0

    for dz in range(3):
        for dy in range(3):
            for dx in range(3):
                k = 9 * dz + 3 * dy + dx
                for i in range(16):
                    put(28 + k * 16 + i, dx * 256 + (dz * 4 + dy) * 16 + i)
                put(k, 896 + dx * 64 + dz * 16 + 3 + dy)
    for lane in range(128):
        put(28 + 27 * 16, 768 + lane)
    put(27, 1152 + 192)
    return table.astype(BF)


def adam(params, moment, second, gradient):
    new_moment = 0.9 * moment + 0.1 * gradient
    new_second = 0.999 * second + 0.001 * gradient * gradient
    new_params = params - 0.01 * new_moment / (jnp.sqrt(new_second) + 1e-08)
    return new_params, new_moment, new_second


def update_encoder(scale, grad_ref, state_ref, table_ref, new_ref, two_ref, one_ref, bias_ref):
    gradient = grad_ref[...] * scale
    new = adam(state_ref[0], state_ref[1], state_ref[2], gradient)
    for n in range(3):
        new_ref[n] = new[n]
    rows = lax.broadcasted_iota(jnp.int32, (64, 128), 0)
    lanes = lax.broadcasted_iota(jnp.int32, (64, 128), 1)
    clean = jnp.where(rows * 128 + lanes < 7376, new[0], 0.0)
    turned = jnp.transpose(clean).astype(BF)
    found = jnp.zeros((16, 1408), F32)
    for group in range(8):
        found = found + mm(turned[group * 16 : (group + 1) * 16], table_ref[group])
    two_ref[...] = shifted_kernels([found[:, dx * 256 : (dx + 1) * 256] for dx in range(3)])
    bias_ref[...] = found[:, 768:896]
    base, bias = found[:, 896:1152], found[:, 1152:1408]
    one_ref[...] = jnp.concatenate(
        [
            (pltpu.roll(base, z * 16 + r, 1) if z + r else base) + bias
            for z in range(2)
            for r in range(8)
        ],
        axis=0,
    ).astype(BF)


def call_update_encoder(scale, grad, state, table):
    return pl.pallas_call(
        lambda *refs: update_encoder(scale, *refs),
        out_shape=[
            jax.ShapeDtypeStruct((3, 64, 128), F32),
            jax.ShapeDtypeStruct((192, 256), BF),
            jax.ShapeDtypeStruct((256, 256), BF),
            jax.ShapeDtypeStruct((16, 128), F32),
        ],
        compiler_params=pltpu.CompilerParams(vmem_limit_bytes=LIMIT),
        name="update_encoder",
    )(grad, state, table)


def volume_windows(odd_ref, near_ref, far_ref, volume_ref, out_ref):
    odd = odd_ref[0]
    not_first, not_last = lane_masks(128)
    for plane in range(8):
        if plane < 2 or plane > 5:
            z = plane if plane < 2 else plane - 6
            low = plane < 2
            near = near_ref[16 + z].astype(F32)
            far = far_ref[16 + z].astype(F32)
            use_near = odd == (1 if low else 0)
            cells = jnp.where(use_near, near, far)
        else:
            cells = volume_ref[plane - 2].astype(F32)
        lateral = (from_left(cells, not_first), cells, from_right(cells, not_last))
        pad = jnp.zeros((4, 128), F32)
        for dx in range(3):
            value = lateral[dx]
            down = jnp.concatenate([pad, value[:124]], axis=0)
            up = jnp.concatenate([value[4:], pad], axis=0)
            out_ref[0, dx, plane] = down.astype(BF).reshape(8, 16, 128)
            out_ref[1, dx, plane] = up.astype(BF).reshape(8, 16, 128)


def call_volume_windows(odd, near, far, volume):
    vmem = pl.BlockSpec(memory_space=pltpu.VMEM)
    return pl.pallas_call(
        volume_windows,
        in_specs=[pl.BlockSpec(memory_space=pltpu.SMEM), vmem, vmem, vmem],
        out_shape=jax.ShapeDtypeStruct((2, 3, 8, 8, 16, 128), BF),
        compiler_params=pltpu.CompilerParams(vmem_limit_bytes=LIMIT),
        name="volume_windows",
    )(odd, near, far, volume)


def encode(inside_ref, one_ref, two_ref, bias_ref, cells_ref, out_ref, first, held):
    step = pl.program_id(0)

    @pl.when(step == 0)
    def _():
        edge = jnp.zeros((6, 1, 16, 128), BF)
        first[:, 0:1] = edge
        first[:, 129:130] = edge
        rows = lax.broadcasted_iota(jnp.int32, (64, 256), 0)
        ones = jnp.where(rows == 0, 1.0, 0.0).astype(BF)
        kernel = one_ref[...]

        def body(j, carry):
            for zp in range(3):
                cells = jnp.concatenate(
                    [
                        jnp.concatenate(
                            [cells_ref[s, dx, 2 * zp + z, j] for s in range(2)], axis=1
                        )
                        for dx in range(3)
                        for z in range(4)
                    ]
                    + [ones],
                    axis=0,
                )
                product = jnp.maximum(mm(kernel, cells), 0.0)
                for s in range(2):
                    part = product[:, s * 128 : (s + 1) * 128].reshape(2, 128, 128)
                    for z in range(2):
                        plane = 2 * zp + z
                        value = part[z]
                        if plane == 0:
                            value = jnp.where(inside_ref[0] == 1, value, 0.0)
                        if plane == 5:
                            value = jnp.where(inside_ref[1] == 1, value, 0.0)
                        first[plane, pl.ds(j * 16 + s * 8 + 1, 8)] = value.astype(BF).reshape(
                            8, 16, 128
                        )
            return carry

        lax.fori_loop(0, 8, body, 0)

    bias = jnp.concatenate([bias_ref[...]] * 4, axis=0)
    planes = [(first, z) for z in range(6)]
    conv_block(
        step, planes, two_ref[...], out_ref, held, lambda value: jnp.maximum(value + bias, 0.0)
    )


def call_encode(inside, one, two, bias, cells):
    whole = lambda shape: pl.BlockSpec(shape, lambda j: (0,) * len(shape))
    return pl.pallas_call(
        encode,
        grid=(8,),
        in_specs=[
            pl.BlockSpec(memory_space=pltpu.SMEM),
            whole((256, 256)),
            whole((192, 256)),
            whole((16, 128)),
            whole((2, 3, 8, 8, 16, 128)),
        ],
        out_specs=pl.BlockSpec((16, 4, 16, 128), lambda j: (0, 0, j, 0)),
        out_shape=jax.ShapeDtypeStruct((16, 4, 128, 128), BF),
        scratch_shapes=[pltpu.VMEM((6, 130, 16, 128), BF), pltpu.VMEM((4, 16, 16, 128), BF)],
        compiler_params=pltpu.CompilerParams(vmem_limit_bytes=LIMIT),
        name="encode",
    )(inside, one, two, bias, cells)


def partner(value, axis, bit):
    count = lax.axis_size(axis)
    return lax.ppermute(value, axis, [(i, i ^ bit) for i in range(count)])


def local(activation, cotangent, volume, dec_weight, enc_grad, params, moment, second):
    act, cot, vol = activation[0], cotangent[0], volume[0, 0]
    space = lax.axis_index("space")
    count = lax.axis_size("space")
    n_dp = lax.axis_size("dp")
    data = lax.axis_index("dp")
    odd = lax.rem(space, 2)
    odd_arg = odd.reshape(1).astype(jnp.int32)

    def boundary(side):
        cot_plane = lax.dynamic_index_in_dim(cot, 3 * side, 1, keepdims=False)
        vol_planes = lax.dynamic_slice_in_dim(vol, 2 * side, 2, 0)
        return jnp.concatenate([cot_plane, vol_planes], axis=0)

    near = lax.ppermute(boundary(1 - odd), "space", [(i, i ^ 1) for i in range(count)])
    pairs = [(i, i + 1) for i in range(1, count - 1, 2)]
    far = lax.ppermute(boundary(odd), "space", pairs + [(b, a) for a, b in pairs])

    enc = jnp.pad(enc_grad[0, 0], (0, 8192 - 7376)).reshape(64, 128)
    pad = lambda value: jnp.pad(value, (0, 2048 - 1786)).reshape(16, 128)
    state = jnp.concatenate([pad(params), pad(moment), pad(second)], axis=0)[None]
    for bit in (1, 2, 4):
        sent = jnp.concatenate([enc, state.reshape(-1, 128)], axis=0)
        got = partner(sent, "dp", bit)
        enc = enc + got[:64]
        state = jnp.concatenate([state, got[64:].reshape(state.shape)], axis=0)
    state = state.reshape(2, 2, 2, 3, 2048)
    for axis, bit in ((0, 4), (1, 2), (2, 1)):
        state = jnp.where((data & bit) != 0, jnp.flip(state, axis), state)
    state = state.reshape(8, 3, 2048)[:, :, :1786].transpose(1, 0, 2).reshape(3, 14288)
    enc_state = jnp.pad(state[:, 6912:], ((0, 0), (0, 8192 - 7376))).reshape(3, 64, 128)

    act_rows, cot_rows = call_rows_first(act, cot)
    dec, rim_rows = call_weight_sum(odd_arg, near, far, act_rows, cot_rows)
    for axis, bit in (("space", 8), ("space", 4)):
        enc = enc + partner(enc, axis, bit)
    both = jnp.concatenate([enc, dec.reshape(96, 128)], axis=0)
    for axis, bit in (("space", 2), ("space", 1)):
        both = both + partner(both, axis, bit)
    enc, dec = both[:64], both[64:]
    grad_input = call_input_grad(dec_weight, cot_rows, rim_rows)[None]

    devices = n_dp * count
    table = jnp.asarray(placement())
    new_enc, two, one, bias = call_update_encoder(1.0 / math.sqrt(devices), enc, enc_state, table)
    cells = call_volume_windows(odd_arg, near, far, vol)
    inside = jnp.stack([space > 0, space < count - 1]).astype(jnp.int32)
    encoded = call_encode(inside, one, two, bias, cells)[None]

    for axis, bit in (("space", 8), ("space", 4), ("dp", 1), ("dp", 2), ("dp", 4)):
        dec = dec + partner(dec, axis, bit)
    voxels = devices * act.shape[1] * act.shape[2] * act.shape[3]
    dec = dec.reshape(3, 16, 4, 4, 16)[:, :, 2::-1, 2::-1]
    dec = dec.transpose(2, 3, 0, 1, 4).reshape(6912) / math.sqrt(voxels)
    new_dec = adam(state[0, :6912], state[1, :6912], state[2, :6912], dec)
    new = [
        jnp.concatenate([new_dec[n], new_enc[n].reshape(8192)[:7376]]) for n in range(3)
    ]
    working = new[0].astype(BF)
    own = [lax.dynamic_slice_in_dim(value, data * 1786, 1786, 0) for value in new]
    return (grad_input, own[0], own[1], own[2], working, encoded)


def solution(mesh):
    in_specs = (
        P("dp", None, "space", None, None),
        P("dp", None, "space", None, None),
        P("dp", None, "space", None, None),
        P(),
        P("dp", "space", None),
        P("dp"),
        P("dp"),
        P("dp"),
    )
    out_specs = (
        P("dp", None, "space", None, None),
        P("dp"),
        P("dp"),
        P("dp"),
        P(),
        P("dp", None, "space", None, None),
    )
    return jax.shard_map(local, mesh=mesh, in_specs=in_specs, out_specs=out_specs, check_vma=False)
```

```python
import functools
import math

import jax
import jax.numpy as jnp
import numpy as np
from jax import lax
from jax.experimental import pallas as pl
from jax.experimental.pallas import tpu as pltpu
from jax.sharding import PartitionSpec as P

BF = jnp.bfloat16
F32 = jnp.float32
LIMIT = 32 * 1024 * 1024


def exchange_matrix():
    rows = lax.broadcasted_iota(jnp.int32, (256, 256), 0)
    cols = lax.broadcasted_iota(jnp.int32, (256, 256), 1)
    return jnp.where(cols == (rows % 16) * 16 + rows // 16, 1.0, 0.0).astype(BF)


def mm(left, right):
    return lax.dot_general(left, right, (((1,), (0,)), ((), ())), preferred_element_type=F32)


def mm_lanes(left, right):
    return lax.dot_general(left, right, (((1,), (1,)), ((), ())), preferred_element_type=F32)


def lane_masks(rows):
    lanes = lax.broadcasted_iota(jnp.int32, (rows, 128), 1)
    return lanes != 0, lanes != 127


def from_left(value, keep):
    return jnp.where(keep, pltpu.roll(value, 1, 1), 0.0)


def from_right(value, keep):
    return jnp.where(keep, pltpu.roll(value, 127, 1), 0.0)


VM = pl.BlockSpec(memory_space=pltpu.VMEM)
HBM = pl.BlockSpec(memory_space=pltpu.HBM)
SM = pl.BlockSpec(memory_space=pltpu.SMEM)


def kernel_call(
    body, name, in_specs, out_shape, scratch=(), micros=1.0, out_specs=None, aliases=None
):
    if out_specs is None:
        out_specs = jax.tree.map(lambda shape: VM, out_shape)
    return pl.pallas_call(
        body,
        in_specs=in_specs,
        out_specs=out_specs,
        out_shape=out_shape,
        input_output_aliases=aliases or {},
        scratch_shapes=list(scratch),
        compiler_params=pltpu.CompilerParams(vmem_limit_bytes=LIMIT),
        cost_estimate=pl.CostEstimate(
            flops=int(micros * 1.15e9), bytes_accessed=int(micros * 3.6e6), transcendentals=0
        ),
        name=name,
    )


def in_hbm(value):
    return pltpu.with_memory_space_constraint(value, pltpu.HBM)


def edges(odd_ref, cot_ref, vol_ref, far_ref, near_ref, planes, slabs, sems):
    odd = odd_ref[0]
    outs = (far_ref, near_ref)
    sides = (odd, 1 - odd)
    copies = []
    for n in range(2):
        pair = (
            pltpu.make_async_copy(cot_ref.at[:, 3 * sides[n]], planes.at[n], sems.at[n]),
            pltpu.make_async_copy(
                vol_ref.at[pl.ds(2 * sides[n], 2)], slabs.at[n], sems.at[2 + n]
            ),
        )
        for copy in pair:
            copy.start()
        copies.append(pair)
    for n in range(2):
        copies[n][0].wait()
        for j in range(8):
            rows = slice(j * 16, (j + 1) * 16)
            outs[n][rows] = jnp.swapaxes(planes[n, :, rows], 0, 1)
        copies[n][1].wait()
        outs[n][128:144] = slabs[n].reshape(16, 16, 128)


def call_edges(odd, cot, vol):
    shape = jax.ShapeDtypeStruct((144, 16, 128), BF)
    return kernel_call(
        edges,
        "edges",
        [SM, HBM, HBM],
        [shape, shape],
        [
            pltpu.VMEM((2, 16, 128, 128), BF),
            pltpu.VMEM((2, 2, 128, 128), BF),
            pltpu.SemaphoreType.DMA((4,)),
        ],
        1.3,
    )(odd, in_hbm(cot), in_hbm(vol))


def lateral(cells):
    zero = jnp.zeros((cells.shape[0], 1), BF)
    left = jnp.concatenate([zero, cells[:, :127]], axis=1)
    right = jnp.concatenate([cells[:, 1:], zero], axis=1)
    return left, cells, right


def aligned(total, rows, keep):
    out = []
    lanes = lax.broadcasted_iota(jnp.int32, (16, 256), 1) // 64
    for dx in range(3):
        summed = None
        for z, (turn, valid) in enumerate(keep):
            for r in range(2):
                start = ((dx * rows + z) * 2 + r) * 16
                part = total[start : start + 16]
                shift = (turn - r * 16) % 256
                if shift:
                    part = pltpu.roll(part, shift, 1)
                if valid is not None:
                    part = jnp.where((lanes >= valid[0]) & (lanes <= valid[1]), part, 0.0)
                summed = part if summed is None else summed + part
        out.append(summed)
    return jnp.concatenate(out, axis=0)


def inner(
    act_hbm, cot_hbm, token_ref, grad_ref, cot_rows, act_edge, act_ref, cot_ref, act_rows, total, sems
):
    def copies(step):
        rows = pl.ds(pl.multiple_of(step * 16, 16), 16)
        return [
            pltpu.make_async_copy(source.at[:, :, rows], target.at[:, :, rows], sems.at[n, step])
            for n, (source, target) in enumerate(((act_hbm, act_ref), (cot_hbm, cot_ref)))
        ]

    for step in range(8):
        for copy in copies(step):
            copy.start()
    edge = jnp.zeros((4, 1, 16, 128), BF)
    cot_rows[:, 0:1] = edge
    cot_rows[:, 129:130] = edge
    total[...] = jnp.zeros_like(total)

    def turn(step):
        for copy in copies(step):
            copy.wait()
        rows = pl.ds(pl.multiple_of(step * 16, 16), 16)
        for z in range(4):
            cot_rows[z, pl.ds(step * 16 + 1, 16)] = jnp.swapaxes(cot_ref[:, z, rows], 0, 1)
            cells = jnp.swapaxes(act_ref[:, z, rows], 0, 1).reshape(256, 128)
            for dx, value in enumerate(lateral(cells)):
                act_rows[dx, z, pl.ds(step * 16, 16)] = value.reshape(16, 16, 128)

    def gather(step):
        left, right = [], []
        for q in range(8):
            base = step * 16 + 2 * q
            left.append(
                jnp.concatenate(
                    [
                        act_rows[dx, z, pl.ds(base, 2)].reshape(32, 128)
                        for dx in range(3)
                        for z in range(4)
                    ],
                    axis=0,
                )
            )
            right.append(window([(cot_rows, z) for z in range(4)], base))
        total[...] += mm_lanes(jnp.concatenate(left, axis=1), jnp.concatenate(right, axis=1))

    turn(0)
    turn(1)

    def body(step, carry):
        turn(step + 2)
        gather(step)
        return carry

    lax.fori_loop(0, 6, body, 0)
    gather(6)
    gather(7)
    grad_ref[...] = aligned(
        total, 4, [(64, (1, 2)), (0, None), (192, None), (128, (0, 1))]
    )
    act_edge[0] = act_rows[:, 0]
    act_edge[1] = act_rows[:, 3]


def call_inner(act, cot, token):
    return kernel_call(
        inner,
        "inner",
        [HBM, HBM, VM],
        [
            jax.ShapeDtypeStruct((48, 256), F32),
            jax.ShapeDtypeStruct((4, 130, 16, 128), BF),
            jax.ShapeDtypeStruct((2, 3, 128, 16, 128), BF),
        ],
        [
            pltpu.VMEM((16, 4, 128, 128), BF),
            pltpu.VMEM((16, 4, 128, 128), BF),
            pltpu.VMEM((3, 4, 128, 16, 128), BF),
            pltpu.VMEM((384, 256), F32),
            pltpu.SemaphoreType.DMA((2, 8)),
        ],
        4.0,
    )(in_hbm(act), in_hbm(cot), token)


def window(planes, base):
    return jnp.concatenate(
        [ref[z, pl.ds(base, 4)].reshape(64, 128) for ref, z in planes], axis=0
    )


def outer(odd_ref, far_ref, near_ref, act_edge, inner_ref, token_ref, grad_ref, rim_ref, total):
    edge = jnp.zeros((2, 1, 16, 128), BF)
    rim_ref[:, 0:1] = edge
    rim_ref[:, 129:130] = edge
    rim_ref[odd_ref[0], 1:129] = far_ref[0:128]
    rim_ref[1 - odd_ref[0], 1:129] = near_ref[0:128]
    total[...] = jnp.zeros_like(total)

    def body(step, carry):
        left, right = [], []
        for q in range(16):
            base = step * 32 + 2 * q
            left.append(
                jnp.concatenate(
                    [
                        act_edge[side, dx, pl.ds(base, 2)].reshape(32, 128)
                        for dx in range(3)
                        for side in range(2)
                    ],
                    axis=0,
                )
            )
            right.append(window([(rim_ref, 0), (rim_ref, 1)], base))
        total[:, 0:128] += mm_lanes(
            jnp.concatenate(left, axis=1), jnp.concatenate(right, axis=1)
        )
        return carry

    lax.fori_loop(0, 4, body, 0)
    grad_ref[...] = inner_ref[...] + aligned(total, 2, [(0, (0, 0)), (64, (2, 2))])


def call_outer(odd, far, near, act_edge, inner_grad, token):
    return kernel_call(
        outer,
        "outer",
        [SM, VM, VM, VM, VM, VM],
        [
            jax.ShapeDtypeStruct((48, 256), F32),
            jax.ShapeDtypeStruct((2, 130, 16, 128), BF),
        ],
        [pltpu.VMEM((192, 256), F32)],
        2.5,
    )(odd, far, near, act_edge, inner_grad, token)


def conv_rows(part, planes, kernel, out_hbm, held, out, sems, finish):
    swap = exchange_matrix()
    not_first, not_last = lane_masks(64)
    first = part * 64

    def compute(pair):
        for block in range(2):
            for q in range(8):
                base = first + pair * 32 + block * 16 + 2 * q
                cells = jnp.concatenate(
                    [window(planes[2 * zt : 2 * zt + 4], base) for zt in range(2)], axis=1
                )
                product = mm(kernel, cells)
                for zt in range(2):
                    piece = product[:, zt * 128 : (zt + 1) * 128]
                    summed = (
                        piece[64:128]
                        + from_left(piece[0:64], not_first)
                        + from_right(piece[128:192], not_last)
                    )
                    rounded = finish(summed).astype(BF).reshape(2, 2, 16, 128)
                    for z in range(2):
                        held[pair, block, 2 * zt + z, 2 * q : 2 * q + 2] = rounded[z]

    def flush(pair):
        for block in range(2):
            rows = slice(pair * 32 + block * 16, pair * 32 + block * 16 + 16)
            for zt in range(2):
                cells = jnp.concatenate(
                    [held[pair, block, 2 * zt + z].reshape(256, 128) for z in range(2)], axis=1
                )
                moved = mm(swap, cells).astype(BF)
                for z in range(2):
                    piece = moved[:, z * 128 : (z + 1) * 128]
                    out[:, 2 * zt + z, rows] = piece.reshape(16, 16, 128)
        copy = pltpu.make_async_copy(
            out.at[:, :, pair * 32 : pair * 32 + 32],
            out_hbm.at[:, :, first + pair * 32 : first + pair * 32 + 32],
            sems.at[pair],
        )
        copy.start()
        return copy

    compute(0)
    compute(1)
    copies = [flush(0), flush(1)]
    for copy in copies:
        copy.wait()


FIELD = jax.ShapeDtypeStruct((16, 4, 128, 128), BF)
HELD = [
    pltpu.VMEM((2, 2, 4, 16, 16, 128), BF),
    pltpu.VMEM((16, 4, 64, 128), BF),
    pltpu.SemaphoreType.DMA((2,)),
]


def shifted_kernels(bases):
    return jnp.concatenate(
        [
            pltpu.roll(base, (z * 4 + r) * 16, 1) if z + r else base
            for base in bases
            for z in range(2)
            for r in range(2)
        ],
        axis=0,
    ).astype(BF)


def input_grad(part, kernel_ref, cot_ref, rim_ref, token_ref, *refs):
    out_ref, held, out, sems = refs[-4:]
    planes = [(rim_ref, 0)] + [(cot_ref, z) for z in range(4)] + [(rim_ref, 1)]
    conv_rows(part, planes, kernel_ref[...], out_ref, held, out, sems, lambda value: value)


def call_input_grad(part, kernel, cot_rows, rim_rows, token, *before):
    return kernel_call(
        functools.partial(input_grad, part),
        f"input_grad_{part}",
        [VM, VM, VM, VM] + [HBM] * len(before),
        FIELD,
        HELD,
        2.2,
        HBM,
        {4: 0} if before else None,
    )(kernel, cot_rows, rim_rows, token, *before)


def placement():
    table = np.zeros((8, 64, 1408), np.float32)

    def put(group, column):
        table[group % 8, group // 8, column] = 1.0

    for dz in range(3):
        for dy in range(3):
            for dx in range(3):
                k = 9 * dz + 3 * dy + dx
                for i in range(16):
                    put(28 + k * 16 + i, dx * 256 + (dz * 4 + dy) * 16 + i)
                put(k, 896 + dx * 64 + dz * 16 + 3 + dy)
    for lane in range(128):
        put(28 + 27 * 16, 768 + lane)
    put(27, 1152 + 192)
    return table.astype(BF)


def adam(params, moment, second, gradient):
    new_moment = 0.9 * moment + 0.1 * gradient
    new_second = 0.999 * second + 0.001 * gradient * gradient
    new_params = params - 0.01 * new_moment / (jnp.sqrt(new_second) + 1e-08)
    return new_params, new_moment, new_second


def update_encoder(scale, grad_ref, state_ref, table_ref, two_ref, one_ref, bias_ref):
    gradient = grad_ref[0:58] * scale
    new = adam(state_ref[0, 54:112], state_ref[1, 54:112], state_ref[2, 54:112], gradient)[0]
    rows = lax.broadcasted_iota(jnp.int32, (58, 128), 0)
    lanes = lax.broadcasted_iota(jnp.int32, (58, 128), 1)
    clean = jnp.where(rows * 128 + lanes < 7376, new, 0.0)
    clean = jnp.concatenate([clean, jnp.zeros((6, 128), F32)], axis=0)
    turned = jnp.transpose(clean).astype(BF)
    found = jnp.zeros((16, 1408), F32)
    for group in range(8):
        found = found + mm(turned[group * 16 : (group + 1) * 16], table_ref[group])
    two_ref[...] = shifted_kernels([found[:, dx * 256 : (dx + 1) * 256] for dx in range(3)])
    bias_ref[...] = found[:, 768:896]
    base, bias = found[:, 896:1152], found[:, 1152:1408]
    one_ref[...] = jnp.concatenate(
        [
            (pltpu.roll(base, z * 16 + r, 1) if z + r else base) + bias
            for z in range(2)
            for r in range(8)
        ],
        axis=0,
    ).astype(BF)


def call_update_encoder(scale, grad, state, table):
    return kernel_call(
        functools.partial(update_encoder, scale),
        "update_encoder",
        [VM, VM, VM],
        [
            jax.ShapeDtypeStruct((192, 256), BF),
            jax.ShapeDtypeStruct((256, 256), BF),
            jax.ShapeDtypeStruct((16, 128), F32),
        ],
        micros=0.6,
    )(grad, state, table)


def flat_state(data_ref, shards_ref, token_ref, out_ref):
    data = data_ref[0]
    lanes = lax.broadcasted_iota(jnp.int32, (16, 128), 1)
    for shard in range(8):
        block = shards_ref[lax.bitwise_xor(data, shard)]
        kept = 128 - 6 * shard
        for n in range(3):
            rows = block[16 * n : 16 * n + 16]
            if shard:
                rows = pltpu.roll(rows, kept, 1)
                start = out_ref[n, 14 * shard - 1 : 14 * shard]
                out_ref[n, 14 * shard - 1 : 14 * shard] = jnp.where(
                    lanes[:1] < kept, start, rows[:1]
                )
            out_ref[n, 14 * shard : 14 * shard + 14] = jnp.where(
                lanes[:14] < kept, rows[:14], rows[1:15]
            )


def call_flat_state(data, shards, token):
    return kernel_call(
        flat_state,
        "flat_state",
        [SM, VM, VM],
        jax.ShapeDtypeStruct((3, 112, 128), F32),
        micros=0.3,
    )(data, shards, token)


def finish(scales, dec_ref, enc_ref, state_ref, grad_ref, work_ref):
    lanes = lax.broadcasted_iota(jnp.int32, (16, 128), 1) // 16
    rows = lax.broadcasted_iota(jnp.int32, (16, 128), 0) % 8
    for dz in range(3):
        for dy in range(3):
            place = ((2 - dz) * 4 + 2 - dy) * 16
            for dx in range(3):
                block = dec_ref[dx * 16 : (dx + 1) * 16]
                if place:
                    block = pltpu.roll(block, 256 - place, 1)
                block = jnp.where(lanes == 0, block[:, :128], 0.0)
                for width in (16, 32, 64):
                    block = block + pltpu.roll(block, width, 1)
                block = jnp.where(lanes == rows, block, 0.0).reshape(2, 8, 128)
                k = 9 * dz + 3 * dy + dx
                grad_ref[2 * k : 2 * k + 2] = jnp.sum(block, axis=1) * scales[0]
    grad_ref[54:112] = enc_ref[0:58] * scales[1]
    new = adam(state_ref[0], state_ref[1], state_ref[2], grad_ref[...])[0]
    work_ref[...] = new.astype(BF)


def call_finish(scales, dec, enc, state):
    return kernel_call(
        functools.partial(finish, scales),
        "finish",
        [VM, VM, VM],
        [jax.ShapeDtypeStruct((112, 128), F32), jax.ShapeDtypeStruct((112, 128), BF)],
    )(dec, enc, state)


def prepare(odd_ref, far_ref, near_ref, volume_ref, weight_ref, token_ref, out_ref, kernel_ref):
    not_first, not_last = lane_masks(128)
    for plane in range(8):
        if plane < 2 or plane > 5:
            z = plane if plane < 2 else plane - 6
            far, near = [
                ref[128 + 8 * z : 136 + 8 * z].reshape(128, 128).astype(F32)
                for ref in (far_ref, near_ref)
            ]
            cells = jnp.where(odd_ref[0] == (0 if plane < 2 else 1), far, near)
        else:
            cells = volume_ref[plane - 2]
        cells = cells.astype(F32)
        sides = (from_left(cells, not_first), cells, from_right(cells, not_last))
        pad = jnp.zeros((4, 128), F32)
        for dx in range(3):
            value = sides[dx]
            down = jnp.concatenate([pad, value[:124]], axis=0)
            up = jnp.concatenate([value[4:], pad], axis=0)
            out_ref[0, dx, plane] = down.astype(BF).reshape(8, 16, 128)
            out_ref[1, dx, plane] = up.astype(BF).reshape(8, 16, 128)
    weight = weight_ref[...].reshape(256, 27)
    weight = jnp.concatenate([weight, jnp.zeros((256, 101), BF)], axis=1)
    taps = lax.broadcasted_iota(jnp.int32, (128, 256), 0)
    columns = lax.broadcasted_iota(jnp.int32, (128, 256), 1)
    dz, dy = columns // 64, columns // 16 % 4
    rows = lax.broadcasted_iota(jnp.int32, (256, 256), 0)
    lanes = lax.broadcasted_iota(jnp.int32, (256, 256), 1)
    same = rows % 16 == lanes % 16
    summing = jnp.where(rows[:16] == lanes[:16] // 16, 1.0, 0.0).astype(BF)
    bases = []
    for dx in range(3):
        wanted = (dz < 3) & (dy < 3) & (taps == 26 - (9 * dz + 3 * dy + dx))
        spread = mm(weight, jnp.where(wanted, 1.0, 0.0).astype(BF))
        bases.append(mm(summing, jnp.where(same, spread, 0.0).astype(BF)))
    kernel_ref[...] = shifted_kernels(bases)


def call_prepare(odd, far, near, volume, weight, token):
    return kernel_call(
        prepare,
        "prepare",
        [SM, VM, VM, VM, VM, VM],
        [
            jax.ShapeDtypeStruct((2, 3, 8, 8, 16, 128), BF),
            jax.ShapeDtypeStruct((192, 256), BF),
        ],
        micros=1.3,
    )(odd, far, near, volume, weight, token)


def first_layer(inside_ref, one_ref, cells_ref, token_ref, first):
    edge = jnp.zeros((6, 1, 16, 128), BF)
    first[:, 0:1] = edge
    first[:, 129:130] = edge
    rows = lax.broadcasted_iota(jnp.int32, (64, 256), 0)
    ones = jnp.where(rows == 0, 1.0, 0.0).astype(BF)
    kernel = one_ref[...]

    def body(half, carry):
        for part in range(4):
            j = half * 4 + part
            for zp in range(3):
                cells = jnp.concatenate(
                    [
                        jnp.concatenate(
                            [cells_ref[s, dx, 2 * zp + z, j] for s in range(2)], axis=1
                        )
                        for dx in range(3)
                        for z in range(4)
                    ]
                    + [ones],
                    axis=0,
                )
                product = jnp.maximum(mm(kernel, cells), 0.0)
                for s in range(2):
                    found = product[:, s * 128 : (s + 1) * 128].reshape(2, 128, 128)
                    for z in range(2):
                        plane = 2 * zp + z
                        value = found[z]
                        if plane == 0:
                            value = jnp.where(inside_ref[0] == 1, value, 0.0)
                        if plane == 5:
                            value = jnp.where(inside_ref[1] == 1, value, 0.0)
                        value = value.astype(BF).reshape(8, 16, 128)
                        first[plane, pl.ds(j * 16 + s * 8 + 1, 8)] = value
        return carry

    lax.fori_loop(0, 2, body, 0)


def call_first_layer(inside, one, cells, token):
    return kernel_call(
        first_layer,
        "first_layer",
        [SM, VM, VM, VM],
        jax.ShapeDtypeStruct((6, 130, 16, 128), BF),
        micros=1.5,
    )(inside, one, cells, token)


def second_layer(part, two_ref, bias_ref, first, token_ref, *refs):
    out_ref, held, out, sems = refs[-4:]
    bias = jnp.concatenate([bias_ref[...]] * 4, axis=0)
    finish = lambda value: jnp.maximum(value + bias, 0.0)
    planes = [(first, z) for z in range(6)]
    conv_rows(part, planes, two_ref[...], out_ref, held, out, sems, finish)


def call_second_layer(part, two, bias, first, token, *before):
    return kernel_call(
        functools.partial(second_layer, part),
        f"second_layer_{part}",
        [VM, VM, VM, VM] + [HBM] * len(before),
        FIELD,
        HELD,
        2.2,
        HBM,
        {4: 0} if before else None,
    )(two, bias, first, token, *before)


def partner(value, axis, bit):
    count = lax.axis_size(axis)
    return lax.ppermute(value, axis, [(i, i ^ bit) for i in range(count)])


def after(*values):
    return lax.optimization_barrier(values)


def local(activation, cotangent, volume, dec_weight, enc_grad, params, moment, second):
    act, cot, vol = activation[0], cotangent[0], volume[0, 0]
    space = lax.axis_index("space")
    count = lax.axis_size("space")
    n_dp = lax.axis_size("dp")
    data = lax.axis_index("dp")
    devices = n_dp * count
    voxels = devices * act.shape[1] * act.shape[2] * act.shape[3]

    odd = lax.rem(space, 2)
    odd_arg = odd.reshape(1).astype(jnp.int32)
    far, near = call_edges(odd_arg, cot, vol)
    pairs = [(i, i + 1) for i in range(1, count - 1, 2)]
    far_in = lax.ppermute(far, "space", pairs + [(b, a) for a, b in pairs])
    near_in = lax.ppermute(near, "space", [(i, i ^ 1) for i in range(count)])

    scales = (1.0 / math.sqrt(voxels), 1.0 / math.sqrt(devices))
    data_arg = data.reshape(1).astype(jnp.int32)
    inside = jnp.stack([space > 0, space < count - 1]).astype(jnp.int32)
    table = jnp.asarray(placement())

    far, enc_grad = after(far, enc_grad)
    enc = jnp.pad(enc_grad[0, 0], (0, 8192 - 7376)).reshape(64, 128)
    pad = lambda value: jnp.pad(value, (0, 2048 - 1786)).reshape(16, 128)
    state = jnp.concatenate([pad(params), pad(moment), pad(second)], axis=0)

    def dp_round(grads, state, bit):
        sent = jnp.concatenate([grads, state], axis=0)
        got = partner(sent, "dp", bit)
        size = grads.shape[0]
        return grads + got[:size], jnp.concatenate([state, got[size:]], axis=0)

    token = enc
    enc, state = dp_round(enc, state, 1)
    inner_grad, cot_rows, act_edge = call_inner(act, cot, token)
    enc, inner_grad = after(enc, inner_grad)
    enc, state = dp_round(enc, state, 2)
    dec, rim_rows = call_outer(odd_arg, far_in, near_in, act_edge, inner_grad, inner_grad)

    both = jnp.concatenate([enc, dec.reshape(96, 128)], axis=0)
    token = both
    both, state = dp_round(both, state, 4)
    cells, kernel = call_prepare(
        odd_arg, far_in, near_in, vol, dec_weight.transpose(1, 2, 0), token
    )
    token = both
    both = both + partner(both, "space", 8)
    grad_input = call_input_grad(0, kernel, cot_rows, rim_rows, token)
    token = both
    both, grad_input = after(both, grad_input)
    both = both + partner(both, "space", 4)
    grad_input = call_input_grad(1, kernel, cot_rows, rim_rows, token, grad_input)
    token = both
    both, grad_input = after(both, grad_input)
    both = both + partner(both, "space", 2)
    state = call_flat_state(data_arg, state.reshape(8, 48, 128), token)
    both, state = after(both, state)
    both = both + partner(both, "space", 1)
    enc, dec = both[:64], both[64:]

    two, one, bias = call_update_encoder(scales[1], enc, state, table)
    first = call_first_layer(inside, one, cells, enc)
    dec = dec + partner(dec, "dp", 1)
    token = dec
    dec, first = after(dec, first)
    dec = dec + partner(dec, "dp", 2)
    encoded = call_second_layer(0, two, bias, first, token)
    encoded = call_second_layer(1, two, bias, first, token, encoded)

    flat, working = call_finish(scales, dec.reshape(48, 256), enc, state)
    working = working.reshape(112 * 128)[:14288]
    own = lax.dynamic_slice_in_dim(flat.reshape(112 * 128), data * 1786, 1786, 0)
    own = adam(params, moment, second, own)
    return (grad_input[None], own[0], own[1], own[2], working, encoded[None])


def solution(mesh):
    in_specs = (
        P("dp", None, "space", None, None),
        P("dp", None, "space", None, None),
        P("dp", None, "space", None, None),
        P(),
        P("dp", "space", None),
        P("dp"),
        P("dp"),
        P("dp"),
    )
    out_specs = (
        P("dp", None, "space", None, None),
        P("dp"),
        P("dp"),
        P("dp"),
        P(),
        P("dp", None, "space", None, None),
    )
    return jax.shard_map(local, mesh=mesh, in_specs=in_specs, out_specs=out_specs, check_vma=False)
```

```python
import functools
import math

import jax
import jax.numpy as jnp
import numpy as np
from jax import lax
from jax.experimental import pallas as pl
from jax.experimental.pallas import tpu as pltpu
from jax.sharding import PartitionSpec as P

BF = jnp.bfloat16
F32 = jnp.float32
LIMIT = 32 * 1024 * 1024


def exchange_matrix():
    rows = lax.broadcasted_iota(jnp.int32, (256, 256), 0)
    cols = lax.broadcasted_iota(jnp.int32, (256, 256), 1)
    return jnp.where(cols == (rows % 16) * 16 + rows // 16, 1.0, 0.0).astype(BF)


def mm(left, right):
    return lax.dot_general(left, right, (((1,), (0,)), ((), ())), preferred_element_type=F32)


def mm_lanes(left, right):
    return lax.dot_general(left, right, (((1,), (1,)), ((), ())), preferred_element_type=F32)


def lane_masks(rows):
    lanes = lax.broadcasted_iota(jnp.int32, (rows, 128), 1)
    return lanes != 0, lanes != 127


def from_left(value, keep):
    return jnp.where(keep, pltpu.roll(value, 1, 1), 0.0)


def from_right(value, keep):
    return jnp.where(keep, pltpu.roll(value, 127, 1), 0.0)


VM = pl.BlockSpec(memory_space=pltpu.VMEM)
HBM = pl.BlockSpec(memory_space=pltpu.HBM)
SM = pl.BlockSpec(memory_space=pltpu.SMEM)


def kernel_call(
    body, name, in_specs, out_shape, scratch=(), micros=1.0, out_specs=None, aliases=None
):
    if out_specs is None:
        out_specs = jax.tree.map(lambda shape: VM, out_shape)
    return pl.pallas_call(
        body,
        in_specs=in_specs,
        out_specs=out_specs,
        out_shape=out_shape,
        input_output_aliases=aliases or {},
        scratch_shapes=list(scratch),
        compiler_params=pltpu.CompilerParams(vmem_limit_bytes=LIMIT),
        cost_estimate=pl.CostEstimate(
            flops=int(micros * 1.15e9), bytes_accessed=int(micros * 3.6e6), transcendentals=0
        ),
        name=name,
    )


def in_hbm(value):
    return pltpu.with_memory_space_constraint(value, pltpu.HBM)


def edges(odd_ref, cot_ref, vol_ref, far_ref, near_ref, planes, slabs, sems):
    odd = odd_ref[0]
    outs = (far_ref, near_ref)
    sides = (odd, 1 - odd)
    copies = []
    for n in range(2):
        pair = (
            pltpu.make_async_copy(cot_ref.at[:, 3 * sides[n]], planes.at[n], sems.at[n]),
            pltpu.make_async_copy(
                vol_ref.at[pl.ds(2 * sides[n], 2)], slabs.at[n], sems.at[2 + n]
            ),
        )
        for copy in pair:
            copy.start()
        copies.append(pair)
    for n in range(2):
        copies[n][0].wait()
        for j in range(8):
            rows = slice(j * 16, (j + 1) * 16)
            outs[n][rows] = jnp.swapaxes(planes[n, :, rows], 0, 1)
        copies[n][1].wait()
        outs[n][128:144] = slabs[n].reshape(16, 16, 128)


def call_edges(odd, cot, vol):
    shape = jax.ShapeDtypeStruct((144, 16, 128), BF)
    return kernel_call(
        edges,
        "edges",
        [SM, HBM, HBM],
        [shape, shape],
        [
            pltpu.VMEM((2, 16, 128, 128), BF),
            pltpu.VMEM((2, 2, 128, 128), BF),
            pltpu.SemaphoreType.DMA((4,)),
        ],
        1.3,
    )(odd, in_hbm(cot), in_hbm(vol))


def lateral(cells):
    zero = jnp.zeros((cells.shape[0], 1), BF)
    left = jnp.concatenate([zero, cells[:, :127]], axis=1)
    right = jnp.concatenate([cells[:, 1:], zero], axis=1)
    return left, cells, right


def aligned(total, rows, keep):
    out = []
    lanes = lax.broadcasted_iota(jnp.int32, (16, 256), 1) // 64
    for dx in range(3):
        summed = None
        for z, (turn, valid) in enumerate(keep):
            for r in range(2):
                start = ((dx * rows + z) * 2 + r) * 16
                part = total[start : start + 16]
                shift = (turn - r * 16) % 256
                if shift:
                    part = pltpu.roll(part, shift, 1)
                if valid is not None:
                    part = jnp.where((lanes >= valid[0]) & (lanes <= valid[1]), part, 0.0)
                summed = part if summed is None else summed + part
        out.append(summed)
    return jnp.concatenate(out, axis=0)


def inner(
    act_hbm, cot_hbm, token_ref, grad_ref, cot_rows, act_edge, act_ref, cot_ref, act_rows, total, sems
):
    def copies(step):
        rows = pl.ds(pl.multiple_of(step * 16, 16), 16)
        return [
            pltpu.make_async_copy(source.at[:, :, rows], target.at[:, :, rows], sems.at[n, step])
            for n, (source, target) in enumerate(((act_hbm, act_ref), (cot_hbm, cot_ref)))
        ]

    for step in range(8):
        for copy in copies(step):
            copy.start()
    edge = jnp.zeros((4, 1, 16, 128), BF)
    cot_rows[:, 0:1] = edge
    cot_rows[:, 129:130] = edge
    total[...] = jnp.zeros_like(total)

    def turn(step):
        for copy in copies(step):
            copy.wait()
        rows = pl.ds(pl.multiple_of(step * 16, 16), 16)
        for z in range(4):
            cot_rows[z, pl.ds(step * 16 + 1, 16)] = jnp.swapaxes(cot_ref[:, z, rows], 0, 1)
            cells = jnp.swapaxes(act_ref[:, z, rows], 0, 1).reshape(256, 128)
            for dx, value in enumerate(lateral(cells)):
                act_rows[dx, z, pl.ds(step * 16, 16)] = value.reshape(16, 16, 128)

    def gather(step):
        left, right = [], []
        for q in range(8):
            base = step * 16 + 2 * q
            left.append(
                jnp.concatenate(
                    [
                        act_rows[dx, z, pl.ds(base, 2)].reshape(32, 128)
                        for dx in range(3)
                        for z in range(4)
                    ],
                    axis=0,
                )
            )
            right.append(window([(cot_rows, z) for z in range(4)], base))
        total[...] += mm_lanes(jnp.concatenate(left, axis=1), jnp.concatenate(right, axis=1))

    turn(0)
    turn(1)

    def body(step, carry):
        turn(step + 2)
        gather(step)
        return carry

    lax.fori_loop(0, 6, body, 0)
    gather(6)
    gather(7)
    grad_ref[...] = aligned(
        total, 4, [(64, (1, 2)), (0, None), (192, None), (128, (0, 1))]
    )
    act_edge[0] = act_rows[:, 0]
    act_edge[1] = act_rows[:, 3]


def call_inner(act, cot, token):
    return kernel_call(
        inner,
        "inner",
        [HBM, HBM, VM],
        [
            jax.ShapeDtypeStruct((48, 256), F32),
            jax.ShapeDtypeStruct((4, 130, 16, 128), BF),
            jax.ShapeDtypeStruct((2, 3, 128, 16, 128), BF),
        ],
        [
            pltpu.VMEM((16, 4, 128, 128), BF),
            pltpu.VMEM((16, 4, 128, 128), BF),
            pltpu.VMEM((3, 4, 128, 16, 128), BF),
            pltpu.VMEM((384, 256), F32),
            pltpu.SemaphoreType.DMA((2, 8)),
        ],
        4.0,
    )(in_hbm(act), in_hbm(cot), token)


def window(planes, base):
    return jnp.concatenate(
        [ref[z, pl.ds(base, 4)].reshape(64, 128) for ref, z in planes], axis=0
    )


def flatten(summed, out_ref):
    lanes = lax.broadcasted_iota(jnp.int32, (8, 128), 1) // 16
    rows = lax.broadcasted_iota(jnp.int32, (8, 128), 0)
    out_ref[48:56] = jnp.zeros((8, 128), F32)
    for dx in range(3):
        for high in range(2):
            for half in range(2):
                start = dx * 16 + high * 8
                value = summed[start : start + 8, half * 128 : (half + 1) * 128]
                for bit in (1, 2, 4):
                    row_on, lane_on = (rows & bit) != 0, (lanes & bit) != 0
                    down = pltpu.roll(pltpu.roll(value, bit, 0), 128 - 16 * bit, 1)
                    up = pltpu.roll(pltpu.roll(value, 8 - bit, 0), 16 * bit, 1)
                    moved = jnp.where(row_on, down, up)
                    value = jnp.where(row_on == lane_on, value, moved)
                for place in range(8):
                    dz, dy = 2 - (half * 2 + place // 4), 2 - place % 4
                    if dz >= 0 and dy >= 0:
                        row = 2 * (9 * dz + 3 * dy + dx) + high
                        out_ref[row : row + 1] = value[place : place + 1]


def outer(odd_ref, far_ref, near_ref, act_edge, inner_ref, token_ref, grad_ref, rim_ref, total):
    edge = jnp.zeros((2, 1, 16, 128), BF)
    rim_ref[:, 0:1] = edge
    rim_ref[:, 129:130] = edge
    rim_ref[odd_ref[0], 1:129] = far_ref[0:128]
    rim_ref[1 - odd_ref[0], 1:129] = near_ref[0:128]
    total[...] = jnp.zeros_like(total)

    def body(step, carry):
        left, right = [], []
        for q in range(16):
            base = step * 32 + 2 * q
            left.append(
                jnp.concatenate(
                    [
                        act_edge[side, dx, pl.ds(base, 2)].reshape(32, 128)
                        for dx in range(3)
                        for side in range(2)
                    ],
                    axis=0,
                )
            )
            right.append(window([(rim_ref, 0), (rim_ref, 1)], base))
        total[:, 0:128] += mm_lanes(
            jnp.concatenate(left, axis=1), jnp.concatenate(right, axis=1)
        )
        return carry

    lax.fori_loop(0, 4, body, 0)
    summed = inner_ref[...] + aligned(total, 2, [(0, (0, 0)), (64, (2, 2))])
    flatten(summed, grad_ref)


def call_outer(odd, far, near, act_edge, inner_grad, token):
    return kernel_call(
        outer,
        "outer",
        [SM, VM, VM, VM, VM, VM],
        [
            jax.ShapeDtypeStruct((56, 128), F32),
            jax.ShapeDtypeStruct((2, 130, 16, 128), BF),
        ],
        [pltpu.VMEM((192, 256), F32)],
        2.5,
    )(odd, far, near, act_edge, inner_grad, token)


def conv_rows(part, planes, kernel, out_hbm, held, out, sems, finish):
    swap = exchange_matrix()
    not_first, not_last = lane_masks(64)
    first = part * 64

    def compute(pair):
        for block in range(2):
            for q in range(8):
                base = first + pair * 32 + block * 16 + 2 * q
                cells = jnp.concatenate(
                    [window(planes[2 * zt : 2 * zt + 4], base) for zt in range(2)], axis=1
                )
                product = mm(kernel, cells)
                for zt in range(2):
                    piece = product[:, zt * 128 : (zt + 1) * 128]
                    summed = (
                        piece[64:128]
                        + from_left(piece[0:64], not_first)
                        + from_right(piece[128:192], not_last)
                    )
                    rounded = finish(summed).astype(BF).reshape(2, 2, 16, 128)
                    for z in range(2):
                        held[pair, block, 2 * zt + z, 2 * q : 2 * q + 2] = rounded[z]

    def flush(pair):
        for block in range(2):
            rows = slice(pair * 32 + block * 16, pair * 32 + block * 16 + 16)
            for zt in range(2):
                cells = jnp.concatenate(
                    [held[pair, block, 2 * zt + z].reshape(256, 128) for z in range(2)], axis=1
                )
                moved = mm(swap, cells).astype(BF)
                for z in range(2):
                    piece = moved[:, z * 128 : (z + 1) * 128]
                    out[:, 2 * zt + z, rows] = piece.reshape(16, 16, 128)
        copy = pltpu.make_async_copy(
            out.at[:, :, pair * 32 : pair * 32 + 32],
            out_hbm.at[:, :, first + pair * 32 : first + pair * 32 + 32],
            sems.at[pair],
        )
        copy.start()
        return copy

    compute(0)
    compute(1)
    copies = [flush(0), flush(1)]
    for copy in copies:
        copy.wait()


FIELD = jax.ShapeDtypeStruct((16, 4, 128, 128), BF)
HELD = [
    pltpu.VMEM((2, 2, 4, 16, 16, 128), BF),
    pltpu.VMEM((16, 4, 64, 128), BF),
    pltpu.SemaphoreType.DMA((2,)),
]


def shifted_kernels(bases):
    return jnp.concatenate(
        [
            pltpu.roll(base, (z * 4 + r) * 16, 1) if z + r else base
            for base in bases
            for z in range(2)
            for r in range(2)
        ],
        axis=0,
    ).astype(BF)


def input_grad(part, kernel_ref, cot_ref, rim_ref, token_ref, *refs):
    out_ref, held, out, sems = refs[-4:]
    planes = [(rim_ref, 0)] + [(cot_ref, z) for z in range(4)] + [(rim_ref, 1)]
    conv_rows(part, planes, kernel_ref[...], out_ref, held, out, sems, lambda value: value)


def call_input_grad(part, kernel, cot_rows, rim_rows, token, *before):
    return kernel_call(
        functools.partial(input_grad, part),
        f"input_grad_{part}",
        [VM, VM, VM, VM] + [HBM] * len(before),
        FIELD,
        HELD,
        2.2,
        HBM,
        {4: 0} if before else None,
    )(kernel, cot_rows, rim_rows, token, *before)


def placement():
    table = np.zeros((8, 64, 1408), np.float32)

    def put(group, column):
        table[group % 8, group // 8, column] = 1.0

    for dz in range(3):
        for dy in range(3):
            for dx in range(3):
                k = 9 * dz + 3 * dy + dx
                for i in range(16):
                    put(28 + k * 16 + i, dx * 256 + (dz * 4 + dy) * 16 + i)
                put(k, 896 + dx * 64 + dz * 16 + 3 + dy)
    for lane in range(128):
        put(28 + 27 * 16, 768 + lane)
    put(27, 1152 + 192)
    return table.astype(BF)


def adam(params, moment, second, gradient):
    new_moment = 0.9 * moment + 0.1 * gradient
    new_second = 0.999 * second + 0.001 * gradient * gradient
    new_params = params - 0.01 * new_moment / (jnp.sqrt(new_second) + 1e-08)
    return new_params, new_moment, new_second


def update_encoder(scale, grad_ref, state_ref, table_ref, two_ref, one_ref, bias_ref):
    gradient = grad_ref[54:112] * scale
    new = adam(state_ref[0, 54:112], state_ref[1, 54:112], state_ref[2, 54:112], gradient)[0]
    rows = lax.broadcasted_iota(jnp.int32, (58, 128), 0)
    lanes = lax.broadcasted_iota(jnp.int32, (58, 128), 1)
    clean = jnp.where(rows * 128 + lanes < 7376, new, 0.0)
    clean = jnp.concatenate([clean, jnp.zeros((6, 128), F32)], axis=0)
    turned = jnp.transpose(clean).astype(BF)
    found = jnp.zeros((16, 1408), F32)
    for group in range(8):
        found = found + mm(turned[group * 16 : (group + 1) * 16], table_ref[group])
    two_ref[...] = shifted_kernels([found[:, dx * 256 : (dx + 1) * 256] for dx in range(3)])
    bias_ref[...] = found[:, 768:896]
    base, bias = found[:, 896:1152], found[:, 1152:1408]
    one_ref[...] = jnp.concatenate(
        [
            (pltpu.roll(base, z * 16 + r, 1) if z + r else base) + bias
            for z in range(2)
            for r in range(8)
        ],
        axis=0,
    ).astype(BF)


def call_update_encoder(scale, grad, state, table):
    return kernel_call(
        functools.partial(update_encoder, scale),
        "update_encoder",
        [VM, VM, VM],
        [
            jax.ShapeDtypeStruct((192, 256), BF),
            jax.ShapeDtypeStruct((256, 256), BF),
            jax.ShapeDtypeStruct((16, 128), F32),
        ],
        micros=0.6,
    )(grad, state, table)


def flat_state(data_ref, shards_ref, token_ref, out_ref):
    data = data_ref[0]
    lanes = lax.broadcasted_iota(jnp.int32, (16, 128), 1)
    for shard in range(8):
        away = lax.bitwise_xor(data, shard)
        block = shards_ref[lax.rem(away, 2) * 4 + lax.bitwise_and(away, 2) + away // 4]
        kept = 128 - 6 * shard
        for n in range(3):
            rows = block[16 * n : 16 * n + 16]
            if shard:
                rows = pltpu.roll(rows, kept, 1)
                start = out_ref[n, 14 * shard - 1 : 14 * shard]
                out_ref[n, 14 * shard - 1 : 14 * shard] = jnp.where(
                    lanes[:1] < kept, start, rows[:1]
                )
            out_ref[n, 14 * shard : 14 * shard + 14] = jnp.where(
                lanes[:14] < kept, rows[:14], rows[1:15]
            )


def call_flat_state(data, shards, token):
    return kernel_call(
        flat_state,
        "flat_state",
        [SM, VM, VM],
        jax.ShapeDtypeStruct((3, 112, 128), F32),
        micros=0.3,
    )(data, shards, token)


def finish(scales, dec_ref, enc_ref, state_ref, grad_ref, work_ref):
    rows = lax.broadcasted_iota(jnp.int32, (112, 128), 0)
    grad_ref[...] = enc_ref[...] * scales[1]
    grad_ref[0:56] = jnp.where(rows[:56] < 54, dec_ref[...] * scales[0], grad_ref[0:56])
    new = adam(state_ref[0], state_ref[1], state_ref[2], grad_ref[...])[0]
    work_ref[...] = new.astype(BF)


def call_finish(scales, dec, enc, state):
    return kernel_call(
        functools.partial(finish, scales),
        "finish",
        [VM, VM, VM],
        [jax.ShapeDtypeStruct((112, 128), F32), jax.ShapeDtypeStruct((112, 128), BF)],
    )(dec, enc, state)


def prepare(odd_ref, far_ref, near_ref, volume_ref, weight_ref, token_ref, out_ref, kernel_ref):
    not_first, not_last = lane_masks(128)
    for plane in range(8):
        if plane < 2 or plane > 5:
            z = plane if plane < 2 else plane - 6
            far, near = [
                ref[128 + 8 * z : 136 + 8 * z].reshape(128, 128).astype(F32)
                for ref in (far_ref, near_ref)
            ]
            cells = jnp.where(odd_ref[0] == (0 if plane < 2 else 1), far, near)
        else:
            cells = volume_ref[plane - 2]
        cells = cells.astype(F32)
        sides = (from_left(cells, not_first), cells, from_right(cells, not_last))
        pad = jnp.zeros((4, 128), F32)
        for dx in range(3):
            value = sides[dx]
            down = jnp.concatenate([pad, value[:124]], axis=0)
            up = jnp.concatenate([value[4:], pad], axis=0)
            out_ref[0, dx, plane] = down.astype(BF).reshape(8, 16, 128)
            out_ref[1, dx, plane] = up.astype(BF).reshape(8, 16, 128)
    weight = weight_ref[...].reshape(256, 27)
    weight = jnp.concatenate([weight, jnp.zeros((256, 101), BF)], axis=1)
    taps = lax.broadcasted_iota(jnp.int32, (128, 256), 0)
    columns = lax.broadcasted_iota(jnp.int32, (128, 256), 1)
    dz, dy = columns // 64, columns // 16 % 4
    rows = lax.broadcasted_iota(jnp.int32, (256, 256), 0)
    lanes = lax.broadcasted_iota(jnp.int32, (256, 256), 1)
    same = rows % 16 == lanes % 16
    summing = jnp.where(rows[:16] == lanes[:16] // 16, 1.0, 0.0).astype(BF)
    bases = []
    for dx in range(3):
        wanted = (dz < 3) & (dy < 3) & (taps == 26 - (9 * dz + 3 * dy + dx))
        spread = mm(weight, jnp.where(wanted, 1.0, 0.0).astype(BF))
        bases.append(mm(summing, jnp.where(same, spread, 0.0).astype(BF)))
    kernel_ref[...] = shifted_kernels(bases)


def call_prepare(odd, far, near, volume, weight, token):
    return kernel_call(
        prepare,
        "prepare",
        [SM, VM, VM, VM, VM, VM],
        [
            jax.ShapeDtypeStruct((2, 3, 8, 8, 16, 128), BF),
            jax.ShapeDtypeStruct((192, 256), BF),
        ],
        micros=1.3,
    )(odd, far, near, volume, weight, token)


def first_layer(inside_ref, one_ref, cells_ref, token_ref, first):
    edge = jnp.zeros((6, 1, 16, 128), BF)
    first[:, 0:1] = edge
    first[:, 129:130] = edge
    rows = lax.broadcasted_iota(jnp.int32, (64, 256), 0)
    ones = jnp.where(rows == 0, 1.0, 0.0).astype(BF)
    kernel = one_ref[...]

    def body(half, carry):
        for part in range(4):
            j = half * 4 + part
            for zp in range(3):
                cells = jnp.concatenate(
                    [
                        jnp.concatenate(
                            [cells_ref[s, dx, 2 * zp + z, j] for s in range(2)], axis=1
                        )
                        for dx in range(3)
                        for z in range(4)
                    ]
                    + [ones],
                    axis=0,
                )
                product = jnp.maximum(mm(kernel, cells), 0.0)
                for s in range(2):
                    found = product[:, s * 128 : (s + 1) * 128].reshape(2, 128, 128)
                    for z in range(2):
                        plane = 2 * zp + z
                        value = found[z]
                        if plane == 0:
                            value = jnp.where(inside_ref[0] == 1, value, 0.0)
                        if plane == 5:
                            value = jnp.where(inside_ref[1] == 1, value, 0.0)
                        value = value.astype(BF).reshape(8, 16, 128)
                        first[plane, pl.ds(j * 16 + s * 8 + 1, 8)] = value
        return carry

    lax.fori_loop(0, 2, body, 0)


def call_first_layer(inside, one, cells, token):
    return kernel_call(
        first_layer,
        "first_layer",
        [SM, VM, VM, VM],
        jax.ShapeDtypeStruct((6, 130, 16, 128), BF),
        micros=1.5,
    )(inside, one, cells, token)


def second_layer(part, two_ref, bias_ref, first, token_ref, *refs):
    out_ref, held, out, sems = refs[-4:]
    bias = jnp.concatenate([bias_ref[...]] * 4, axis=0)
    finish = lambda value: jnp.maximum(value + bias, 0.0)
    planes = [(first, z) for z in range(6)]
    conv_rows(part, planes, two_ref[...], out_ref, held, out, sems, finish)


def call_second_layer(part, two, bias, first, token, *before):
    return kernel_call(
        functools.partial(second_layer, part),
        f"second_layer_{part}",
        [VM, VM, VM, VM] + [HBM] * len(before),
        FIELD,
        HELD,
        2.2,
        HBM,
        {4: 0} if before else None,
    )(two, bias, first, token, *before)


def partner(value, axis, bit):
    count = lax.axis_size(axis)
    return lax.ppermute(value, axis, [(i, i ^ bit) for i in range(count)])


def four(value, first, second):
    count = lax.axis_size("dp") * lax.axis_size("space")
    one, two, three = [
        lax.ppermute(value, ("dp", "space"), [(i, i ^ bits) for i in range(count)])
        for bits in (first, second, first ^ second)
    ]
    return (value + one) + (two + three)


def after(*values):
    return lax.optimization_barrier(values)


def local(activation, cotangent, volume, dec_weight, enc_grad, params, moment, second):
    act, cot, vol = activation[0], cotangent[0], volume[0, 0]
    space = lax.axis_index("space")
    count = lax.axis_size("space")
    n_dp = lax.axis_size("dp")
    data = lax.axis_index("dp")
    devices = n_dp * count
    voxels = devices * act.shape[1] * act.shape[2] * act.shape[3]

    odd = lax.rem(space, 2)
    odd_arg = odd.reshape(1).astype(jnp.int32)
    scales = (1.0 / math.sqrt(voxels), 1.0 / math.sqrt(devices))
    data_arg = data.reshape(1).astype(jnp.int32)
    inside = jnp.stack([space > 0, space < count - 1]).astype(jnp.int32)
    table = jnp.asarray(placement())

    own_start = data.astype(jnp.uint32) * 1786
    odd_arg, data_arg, own_start, inside, cot = after(odd_arg, data_arg, own_start, inside, cot)
    far, near = call_edges(odd_arg, cot, vol)
    pairs = [(i, i + 1) for i in range(1, count - 1, 2)]
    far_in = lax.ppermute(far, "space", pairs + [(b, a) for a, b in pairs])
    near_in = partner(near, "space", 1)

    far, enc_grad = after(far, enc_grad)
    enc = jnp.pad(enc_grad[0, 0], (0, 8192 - 7376)).reshape(64, 128)
    pad = lambda value: jnp.pad(value, (0, 2048 - 1786)).reshape(16, 128)
    state = jnp.concatenate([pad(params), pad(moment), pad(second)], axis=0)

    def state_round(enc, state, bit):
        return partner(jnp.concatenate([enc, state], axis=0), "dp", bit)

    def joined(enc, state, got):
        return enc + got[:64], jnp.concatenate([state, got[64:]], axis=0)

    enc = enc + partner(enc, "space", 1)
    got = state_round(enc, state, 4)
    inner_grad, cot_rows, act_edge = call_inner(act, cot, enc)
    got, inner_grad = after(got, inner_grad)
    enc, state = joined(enc, state, got)
    got = state_round(enc, state, 2)
    dec, rim_rows = call_outer(odd_arg, far_in, near_in, act_edge, inner_grad, enc)
    got, dec = after(got, dec)
    enc, state = joined(enc, state, got)

    both = jnp.concatenate([dec[:54], enc[:58]], axis=0)
    token = both
    both = four(both, count, 8)
    cells, kernel = call_prepare(
        odd_arg, far_in, near_in, vol, dec_weight.transpose(1, 2, 0), token
    )
    grad_input = call_input_grad(0, kernel, cot_rows, rim_rows, token)
    both, grad_input = after(both, grad_input)
    token = both
    both = four(both, 2, 4)
    state = jnp.concatenate([state, partner(state, "dp", 1)], axis=0)
    grad_input = call_input_grad(1, kernel, cot_rows, rim_rows, token, grad_input)
    both, grad_input = after(both, grad_input)
    state = call_flat_state(data_arg, state.reshape(8, 48, 128), token)

    two, one, bias = call_update_encoder(scales[1], both, state, table)
    first = call_first_layer(inside, one, cells, both)
    dec = both[:56]
    dec = dec + partner(dec, "dp", 2)
    token = dec
    dec, first = after(dec, first)
    dec = dec + partner(dec, "dp", 4)
    encoded = call_second_layer(0, two, bias, first, token)
    dec, encoded = after(dec, encoded)
    dec = dec + partner(dec, "space", 1)
    encoded = call_second_layer(1, two, bias, first, token, encoded)

    flat, working = call_finish(scales, dec, both, state)
    working = working.reshape(112 * 128)[:14288]
    own = lax.dynamic_slice(flat.reshape(112 * 128), (own_start,), (1786,))
    own = adam(params, moment, second, own)
    return (grad_input[None], own[0], own[1], own[2], working, encoded[None])


def solution(mesh):
    in_specs = (
        P("dp", None, "space", None, None),
        P("dp", None, "space", None, None),
        P("dp", None, "space", None, None),
        P(),
        P("dp", "space", None),
        P("dp"),
        P("dp"),
        P("dp"),
    )
    out_specs = (
        P("dp", None, "space", None, None),
        P("dp"),
        P("dp"),
        P("dp"),
        P(),
        P("dp", None, "space", None, None),
    )
    return jax.shard_map(local, mesh=mesh, in_specs=in_specs, out_specs=out_specs, check_vma=False)
```

```python
import functools
import math

import jax
import jax.numpy as jnp
import numpy as np
from jax import lax
from jax.experimental import pallas as pl
from jax.experimental.pallas import tpu as pltpu
from jax.sharding import PartitionSpec as P

BF = jnp.bfloat16
F32 = jnp.float32
LIMIT = 32 * 1024 * 1024


def exchange_matrix():
    rows = lax.broadcasted_iota(jnp.int32, (256, 256), 0)
    cols = lax.broadcasted_iota(jnp.int32, (256, 256), 1)
    return jnp.where(cols == (rows % 16) * 16 + rows // 16, 1.0, 0.0).astype(BF)


def mm(left, right):
    return lax.dot_general(left, right, (((1,), (0,)), ((), ())), preferred_element_type=F32)


def mm_lanes(left, right):
    return lax.dot_general(left, right, (((1,), (1,)), ((), ())), preferred_element_type=F32)


def lane_masks(rows):
    lanes = lax.broadcasted_iota(jnp.int32, (rows, 128), 1)
    return lanes != 0, lanes != 127


def from_left(value, keep):
    return jnp.where(keep, pltpu.roll(value, 1, 1), 0.0)


def from_right(value, keep):
    return jnp.where(keep, pltpu.roll(value, 127, 1), 0.0)


VM = pl.BlockSpec(memory_space=pltpu.VMEM)
HBM = pl.BlockSpec(memory_space=pltpu.HBM)


def kernel_call(
    body, name, in_specs, out_shape, scratch=(), micros=1.0, out_specs=None, aliases=None
):
    if out_specs is None:
        out_specs = jax.tree.map(lambda shape: VM, out_shape)
    return pl.pallas_call(
        body,
        in_specs=in_specs,
        out_specs=out_specs,
        out_shape=out_shape,
        input_output_aliases=aliases or {},
        scratch_shapes=list(scratch),
        compiler_params=pltpu.CompilerParams(vmem_limit_bytes=LIMIT),
        cost_estimate=pl.CostEstimate(
            flops=int(micros * 1.15e9), bytes_accessed=int(micros * 3.6e6), transcendentals=0
        ),
        name=name,
    )


def in_hbm(value):
    return pltpu.with_memory_space_constraint(value, pltpu.HBM)


def odd_place():
    return lax.rem(lax.axis_index("space"), 2)


def edges(cot_ref, vol_ref, far_ref, near_ref, planes, slabs, sems):
    odd = odd_place()
    outs = (far_ref, near_ref)
    sides = (odd, 1 - odd)
    copies = []
    for n in range(2):
        pair = (
            pltpu.make_async_copy(cot_ref.at[:, 3 * sides[n]], planes.at[n], sems.at[n]),
            pltpu.make_async_copy(
                vol_ref.at[pl.ds(2 * sides[n], 2)], slabs.at[n], sems.at[2 + n]
            ),
        )
        for copy in pair:
            copy.start()
        copies.append(pair)
    for n in range(2):
        copies[n][0].wait()
        for j in range(8):
            rows = slice(j * 16, (j + 1) * 16)
            outs[n][rows] = jnp.swapaxes(planes[n, :, rows], 0, 1)
        copies[n][1].wait()
        outs[n][128:144] = slabs[n].reshape(16, 16, 128)


def call_edges(cot, vol):
    shape = jax.ShapeDtypeStruct((144, 16, 128), BF)
    return kernel_call(
        edges,
        "edges",
        [HBM, HBM],
        [shape, shape],
        [
            pltpu.VMEM((2, 16, 128, 128), BF),
            pltpu.VMEM((2, 2, 128, 128), BF),
            pltpu.SemaphoreType.DMA((4,)),
        ],
        1.3,
    )(in_hbm(cot), in_hbm(vol))


def lateral(cells):
    zero = jnp.zeros((cells.shape[0], 1), BF)
    left = jnp.concatenate([zero, cells[:, :127]], axis=1)
    right = jnp.concatenate([cells[:, 1:], zero], axis=1)
    return left, cells, right


def aligned(total, rows, keep):
    out = []
    lanes = lax.broadcasted_iota(jnp.int32, (16, 256), 1) // 64
    for dx in range(3):
        summed = None
        for z, (turn, valid) in enumerate(keep):
            for r in range(2):
                start = ((dx * rows + z) * 2 + r) * 16
                part = total[start : start + 16]
                shift = (turn - r * 16) % 256
                if shift:
                    part = pltpu.roll(part, shift, 1)
                if valid is not None:
                    part = jnp.where((lanes >= valid[0]) & (lanes <= valid[1]), part, 0.0)
                summed = part if summed is None else summed + part
        out.append(summed)
    return jnp.concatenate(out, axis=0)


def inner(act_ref, cot_ref, token_ref, grad_ref, cot_rows, act_edge, act_rows, total):
    edge = jnp.zeros((4, 1, 16, 128), BF)
    cot_rows[:, 0:1] = edge
    cot_rows[:, 129:130] = edge
    total[...] = jnp.zeros_like(total)

    def turn(step):
        rows = pl.ds(pl.multiple_of(step * 16, 16), 16)
        for z in range(4):
            cot_rows[z, pl.ds(step * 16 + 1, 16)] = jnp.swapaxes(cot_ref[:, z, rows], 0, 1)
            cells = jnp.swapaxes(act_ref[:, z, rows], 0, 1).reshape(256, 128)
            for dx, value in enumerate(lateral(cells)):
                act_rows[dx, z, pl.ds(step * 16, 16)] = value.reshape(16, 16, 128)

    def gather(step):
        left, right = [], []
        for q in range(8):
            base = step * 16 + 2 * q
            left.append(
                jnp.concatenate(
                    [
                        act_rows[dx, z, pl.ds(base, 2)].reshape(32, 128)
                        for dx in range(3)
                        for z in range(4)
                    ],
                    axis=0,
                )
            )
            right.append(window([(cot_rows, z) for z in range(4)], base))
        total[...] += mm_lanes(jnp.concatenate(left, axis=1), jnp.concatenate(right, axis=1))

    turn(0)
    turn(1)

    def body(pair, carry):
        for step in (2 * pair, 2 * pair + 1):
            turn(step + 2)
            gather(step)
        return carry

    lax.fori_loop(0, 3, body, 0)
    gather(6)
    gather(7)
    grad_ref[...] = aligned(
        total, 4, [(64, (1, 2)), (0, None), (192, None), (128, (0, 1))]
    )
    act_edge[0] = act_rows[:, 0]
    act_edge[1] = act_rows[:, 3]


def call_inner(act, cot, token):
    return kernel_call(
        inner,
        "inner",
        [VM, VM, VM],
        [
            jax.ShapeDtypeStruct((48, 256), F32),
            jax.ShapeDtypeStruct((4, 130, 16, 128), BF),
            jax.ShapeDtypeStruct((2, 3, 128, 16, 128), BF),
        ],
        [
            pltpu.VMEM((3, 4, 128, 16, 128), BF),
            pltpu.VMEM((384, 256), F32),
        ],
        4.0,
    )(act, cot, token)


def window(planes, base):
    return jnp.concatenate(
        [ref[z, pl.ds(base, 4)].reshape(64, 128) for ref, z in planes], axis=0
    )


def flatten(summed, out_ref):
    lanes = lax.broadcasted_iota(jnp.int32, (8, 128), 1) // 16
    rows = lax.broadcasted_iota(jnp.int32, (8, 128), 0)
    out_ref[48:56] = jnp.zeros((8, 128), F32)
    for dx in range(3):
        for high in range(2):
            for half in range(2):
                start = dx * 16 + high * 8
                value = summed[start : start + 8, half * 128 : (half + 1) * 128]
                for bit in (1, 2, 4):
                    row_on, lane_on = (rows & bit) != 0, (lanes & bit) != 0
                    down = pltpu.roll(pltpu.roll(value, bit, 0), 128 - 16 * bit, 1)
                    up = pltpu.roll(pltpu.roll(value, 8 - bit, 0), 16 * bit, 1)
                    moved = jnp.where(row_on, down, up)
                    value = jnp.where(row_on == lane_on, value, moved)
                for place in range(8):
                    dz, dy = 2 - (half * 2 + place // 4), 2 - place % 4
                    if dz >= 0 and dy >= 0:
                        row = 2 * (9 * dz + 3 * dy + dx) + high
                        out_ref[row : row + 1] = value[place : place + 1]


def outer(far_ref, near_ref, act_edge, inner_ref, token_ref, grad_ref, rim_ref, total):
    edge = jnp.zeros((2, 1, 16, 128), BF)
    rim_ref[:, 0:1] = edge
    rim_ref[:, 129:130] = edge
    rim_ref[odd_place(), 1:129] = far_ref[0:128]
    rim_ref[1 - odd_place(), 1:129] = near_ref[0:128]
    total[...] = jnp.zeros_like(total)

    def body(step, carry):
        left, right = [], []
        for q in range(32):
            base = step * 64 + 2 * q
            left.append(
                jnp.concatenate(
                    [
                        act_edge[side, dx, pl.ds(base, 2)].reshape(32, 128)
                        for dx in range(3)
                        for side in range(2)
                    ],
                    axis=0,
                )
            )
            right.append(window([(rim_ref, 0), (rim_ref, 1)], base))
        total[:, 0:128] += mm_lanes(
            jnp.concatenate(left, axis=1), jnp.concatenate(right, axis=1)
        )
        return carry

    lax.fori_loop(0, 2, body, 0)
    summed = inner_ref[...] + aligned(total, 2, [(0, (0, 0)), (64, (2, 2))])
    flatten(summed, grad_ref)


def call_outer(far, near, act_edge, inner_grad, token):
    return kernel_call(
        outer,
        "outer",
        [VM, VM, VM, VM, VM],
        [
            jax.ShapeDtypeStruct((56, 128), F32),
            jax.ShapeDtypeStruct((2, 130, 16, 128), BF),
        ],
        [pltpu.VMEM((192, 256), F32)],
        2.5,
    )(far, near, act_edge, inner_grad, token)


def conv_rows(blocks, planes, kernel, out_hbm, held, out, sems, finish):
    swap = exchange_matrix()
    not_first, not_last = lane_masks(64)

    def compute(block):
        for q in range(8):
            base = block * 16 + 2 * q
            cells = jnp.concatenate(
                [window(planes[2 * zt : 2 * zt + 4], base) for zt in range(2)], axis=1
            )
            product = mm(kernel, cells)
            for zt in range(2):
                piece = product[:, zt * 128 : (zt + 1) * 128]
                summed = (
                    piece[64:128]
                    + from_left(piece[0:64], not_first)
                    + from_right(piece[128:192], not_last)
                )
                rounded = finish(summed).astype(BF).reshape(2, 2, 16, 128)
                for z in range(2):
                    held[block % 4, 2 * zt + z, 2 * q : 2 * q + 2] = rounded[z]

    def flush(block):
        rows = slice(block * 16, block * 16 + 16)
        for zt in range(2):
            cells = jnp.concatenate(
                [held[block % 4, 2 * zt + z].reshape(256, 128) for z in range(2)], axis=1
            )
            moved = mm(swap, cells).astype(BF)
            for z in range(2):
                piece = moved[:, z * 128 : (z + 1) * 128]
                out[:, 2 * zt + z, rows] = piece.reshape(16, 16, 128)
        copy = pltpu.make_async_copy(out.at[:, :, rows], out_hbm.at[:, :, rows], sems.at[block])
        copy.start()
        return copy

    copies = []
    for place, block in enumerate(blocks):
        compute(block)
        if place % 2 and place > 1:
            copies += [flush(blocks[place - 3]), flush(blocks[place - 2])]
    copies += [flush(block) for block in blocks[-2:]]
    for copy in copies:
        copy.wait()


FIELD = jax.ShapeDtypeStruct((16, 4, 128, 128), BF)
HELD = [
    pltpu.VMEM((4, 4, 16, 16, 128), BF),
    pltpu.VMEM((16, 4, 128, 128), BF),
    pltpu.SemaphoreType.DMA((8,)),
]


def shifted_kernels(bases):
    return jnp.concatenate(
        [
            pltpu.roll(base, (z * 4 + r) * 16, 1) if z + r else base
            for base in bases
            for z in range(2)
            for r in range(2)
        ],
        axis=0,
    ).astype(BF)


def input_grad(part, kernel_ref, cot_ref, rim_ref, token_ref, *refs):
    out_ref, held, out, sems = refs[-4:]
    planes = [(rim_ref, 0)] + [(cot_ref, z) for z in range(4)] + [(rim_ref, 1)]
    blocks = range(4 * part, 4 * part + 4)
    conv_rows(blocks, planes, kernel_ref[...], out_ref, held, out, sems, lambda value: value)


def call_input_grad(part, kernel, cot_rows, rim_rows, token, *before):
    return kernel_call(
        functools.partial(input_grad, part),
        f"input_grad_{part}",
        [VM, VM, VM, VM] + [HBM] * len(before),
        FIELD,
        HELD,
        2.2,
        HBM,
        {4: 0} if before else None,
    )(kernel, cot_rows, rim_rows, token, *before)


def placement():
    table = np.zeros((8, 64, 1408), np.float32)

    def put(group, column):
        table[group % 8, group // 8, column] = 1.0

    for dz in range(3):
        for dy in range(3):
            for dx in range(3):
                k = 9 * dz + 3 * dy + dx
                for i in range(16):
                    put(28 + k * 16 + i, dx * 256 + (dz * 4 + dy) * 16 + i)
                put(k, 896 + dx * 64 + dz * 16 + 3 + dy)
    for lane in range(128):
        put(28 + 27 * 16, 768 + lane)
    put(27, 1152 + 192)
    return table.astype(BF)


def adam(params, moment, second, gradient):
    new_moment = 0.9 * moment + 0.1 * gradient
    new_second = 0.999 * second + 0.001 * gradient * gradient
    new_params = params - 0.01 * new_moment / (jnp.sqrt(new_second) + 1e-08)
    return new_params, new_moment, new_second


def update_encoder(scale, grad_ref, state_ref, table_ref, two_ref, one_ref, bias_ref):
    gradient = grad_ref[54:112] * scale
    new = adam(state_ref[0, 54:112], state_ref[1, 54:112], state_ref[2, 54:112], gradient)[0]
    rows = lax.broadcasted_iota(jnp.int32, (58, 128), 0)
    lanes = lax.broadcasted_iota(jnp.int32, (58, 128), 1)
    clean = jnp.where(rows * 128 + lanes < 7376, new, 0.0)
    clean = jnp.concatenate([clean, jnp.zeros((6, 128), F32)], axis=0)
    turned = jnp.transpose(clean).astype(BF)
    found = jnp.zeros((16, 1408), F32)
    for group in range(8):
        found = found + mm(turned[group * 16 : (group + 1) * 16], table_ref[group])
    two_ref[...] = shifted_kernels([found[:, dx * 256 : (dx + 1) * 256] for dx in range(3)])
    bias_ref[...] = found[:, 768:896]
    base, bias = found[:, 896:1152], found[:, 1152:1408]
    one_ref[...] = jnp.concatenate(
        [
            (pltpu.roll(base, z * 16 + r, 1) if z + r else base) + bias
            for z in range(2)
            for r in range(8)
        ],
        axis=0,
    ).astype(BF)


def call_update_encoder(scale, grad, state, table):
    return kernel_call(
        functools.partial(update_encoder, scale),
        "update_encoder",
        [VM, VM, VM],
        [
            jax.ShapeDtypeStruct((192, 256), BF),
            jax.ShapeDtypeStruct((256, 256), BF),
            jax.ShapeDtypeStruct((16, 128), F32),
        ],
        micros=0.6,
    )(grad, state, table)


def gather_state(both_ref, got_ref, half_ref, other_ref, sum_ref, out_ref):
    sum_ref[...] = both_ref[...] + got_ref[0:112]
    data = lax.axis_index("dp")
    odd = odd_place()
    lanes = lax.broadcasted_iota(jnp.int32, (16, 128), 1)
    for shard in range(8):
        away = lax.bitwise_xor(data, shard)
        slot = lax.bitwise_and(away, 2) + away // 4
        start = pl.multiple_of(48 * slot, 48)
        kept = 128 - 6 * shard
        for n in range(3):
            span = pl.ds(start + 16 * n, 16)
            there = pl.ds(start + 112 + 16 * n, 16)
            rows = jnp.where(odd == 1, got_ref[there], other_ref[span])
            rows = jnp.where(lax.rem(away, 2) == 1, rows, half_ref[span])
            if shard:
                rows = pltpu.roll(rows, kept, 1)
                before = out_ref[n, 14 * shard - 1 : 14 * shard]
                out_ref[n, 14 * shard - 1 : 14 * shard] = jnp.where(
                    lanes[:1] < kept, before, rows[:1]
                )
            out_ref[n, 14 * shard : 14 * shard + 14] = jnp.where(
                lanes[:14] < kept, rows[:14], rows[1:15]
            )


def call_gather_state(both, got, half, other):
    return kernel_call(
        gather_state,
        "gather_state",
        [VM, VM, VM, VM],
        [jax.ShapeDtypeStruct((112, 128), F32), jax.ShapeDtypeStruct((3, 112, 128), F32)],
        micros=0.3,
    )(both, got, half, other)


def merge(dec_ref, enc_ref, got_ref, state_ref, both_ref, sent_ref, all_ref):
    both_ref[0:54] = dec_ref[0:54]
    both_ref[54:112] = enc_ref[0:58] + got_ref[0:58]
    sent_ref[0:112] = both_ref[...]
    for out, first in ((sent_ref, 112), (all_ref, 0)):
        out[first : first + 96] = state_ref[...]
        out[first + 96 : first + 192] = got_ref[64:160]


def call_merge(dec, enc, got, state):
    return kernel_call(
        merge,
        "merge",
        [VM, VM, VM, VM],
        [jax.ShapeDtypeStruct((rows, 128), F32) for rows in (112, 304, 192)],
        micros=0.2,
    )(dec, enc, got, state)


def finish(scales, dec_ref, enc_ref, state_ref, own_ref, *refs):
    work_ref, *own_refs, flat = refs
    rows = lax.broadcasted_iota(jnp.int32, (112, 128), 0)
    gradient = enc_ref[...] * scales[1]
    dec = jnp.concatenate([dec_ref[...], jnp.zeros((56, 128), F32)], axis=0) * scales[0]
    gradient = jnp.where(rows < 54, dec, gradient)
    work_ref[...] = adam(state_ref[0], state_ref[1], state_ref[2], gradient)[0].astype(BF)
    flat[0:8] = jnp.zeros((8, 128), F32)
    flat[8:120] = gradient
    data = lax.axis_index("dp")
    turned = pltpu.roll(flat[pl.ds(7 + 14 * data, 15)], 6 * data, 1)
    lanes = lax.broadcasted_iota(jnp.int32, (14, 128), 1)
    own = jnp.where(lanes >= 6 * data, turned[1:15], turned[0:14])
    new = adam(own_ref[0:14], own_ref[16:30], own_ref[32:46], own)
    for value, out in zip(new, own_refs):
        for row in range(14):
            width = min(128, 1786 - 128 * row)
            out[pl.ds(128 * row, width)] = value[row][:width]


def call_finish(scales, dec, enc, state, own):
    shard = jax.ShapeDtypeStruct((1786,), F32)
    return kernel_call(
        functools.partial(finish, scales),
        "finish",
        [VM, VM, VM, VM],
        [jax.ShapeDtypeStruct((112, 128), BF), shard, shard, shard],
        [pltpu.VMEM((120, 128), F32)],
    )(dec, enc, state, own)


def volume_windows(far_ref, near_ref, volume_ref, token_ref, out_ref):
    not_first, not_last = lane_masks(128)
    odd = odd_place()
    for plane in range(8):
        if plane < 2 or plane > 5:
            z = plane if plane < 2 else plane - 6
            far, near = [
                ref[start : start + 8].reshape(128, 128).astype(F32)
                for ref, start in ((far_ref, 128 + 8 * z), (near_ref, 128 + 8 * z))
            ]
            cells = jnp.where(odd == (0 if plane < 2 else 1), far, near)
        else:
            cells = volume_ref[plane - 2]
        cells = cells.astype(F32)
        sides = (from_left(cells, not_first), cells, from_right(cells, not_last))
        pad = jnp.zeros((4, 128), F32)
        for dx in range(3):
            value = sides[dx]
            down = jnp.concatenate([pad, value[:124]], axis=0)
            up = jnp.concatenate([value[4:], pad], axis=0)
            out_ref[0, dx, plane] = down.astype(BF).reshape(8, 16, 128)
            out_ref[1, dx, plane] = up.astype(BF).reshape(8, 16, 128)


def call_volume_windows(far, near, volume, token):
    return kernel_call(
        volume_windows,
        "volume_windows",
        [VM, VM, VM, VM],
        jax.ShapeDtypeStruct((2, 3, 8, 8, 16, 128), BF),
        micros=0.5,
    )(far, near, volume, token)


def turn_weights(weight_ref, token_ref, kernel_ref):
    weight = weight_ref[...].reshape(256, 27)
    weight = jnp.concatenate([weight, jnp.zeros((256, 101), BF)], axis=1)
    taps = lax.broadcasted_iota(jnp.int32, (128, 256), 0)
    columns = lax.broadcasted_iota(jnp.int32, (128, 256), 1)
    dz, dy = columns // 64, columns // 16 % 4
    rows = lax.broadcasted_iota(jnp.int32, (256, 256), 0)
    lanes = lax.broadcasted_iota(jnp.int32, (256, 256), 1)
    same = rows % 16 == lanes % 16
    summing = jnp.where(rows[:16] == lanes[:16] // 16, 1.0, 0.0).astype(BF)
    bases = []
    for dx in range(3):
        wanted = (dz < 3) & (dy < 3) & (taps == 26 - (9 * dz + 3 * dy + dx))
        spread = mm(weight, jnp.where(wanted, 1.0, 0.0).astype(BF))
        bases.append(mm(summing, jnp.where(same, spread, 0.0).astype(BF)))
    kernel_ref[...] = shifted_kernels(bases)


def call_turn_weights(weight, token):
    return kernel_call(
        turn_weights,
        "turn_weights",
        [VM, VM],
        jax.ShapeDtypeStruct((192, 256), BF),
        micros=0.5,
    )(weight, token)


def first_layer(one_ref, cells_ref, token_ref, first):
    space = lax.axis_index("space")
    edge = jnp.zeros((6, 1, 16, 128), BF)
    first[:, 0:1] = edge
    first[:, 129:130] = edge
    rows = lax.broadcasted_iota(jnp.int32, (64, 256), 0)
    ones = jnp.where(rows == 0, 1.0, 0.0).astype(BF)
    kernel = one_ref[...]

    def body(half, carry):
        for part in range(4):
            j = half * 4 + part
            for zp in range(3):
                cells = jnp.concatenate(
                    [
                        jnp.concatenate(
                            [cells_ref[s, dx, 2 * zp + z, j] for s in range(2)], axis=1
                        )
                        for dx in range(3)
                        for z in range(4)
                    ]
                    + [ones],
                    axis=0,
                )
                product = jnp.maximum(mm(kernel, cells), 0.0)
                for s in range(2):
                    found = product[:, s * 128 : (s + 1) * 128].reshape(2, 128, 128)
                    for z in range(2):
                        plane = 2 * zp + z
                        value = found[z]
                        if plane == 0:
                            value = jnp.where(space > 0, value, 0.0)
                        if plane == 5:
                            value = jnp.where(space < lax.axis_size("space") - 1, value, 0.0)
                        value = value.astype(BF).reshape(8, 16, 128)
                        first[plane, pl.ds(j * 16 + s * 8 + 1, 8)] = value
        return carry

    lax.fori_loop(0, 2, body, 0)


def call_first_layer(one, cells, token):
    return kernel_call(
        first_layer,
        "first_layer",
        [VM, VM, VM],
        jax.ShapeDtypeStruct((6, 130, 16, 128), BF),
        micros=1.5,
    )(one, cells, token)


def second_layer(two_ref, bias_ref, first, token_ref, out_ref, held, out, sems):
    bias = jnp.concatenate([bias_ref[...]] * 4, axis=0)
    finish = lambda value: jnp.maximum(value + bias, 0.0)
    planes = [(first, z) for z in range(6)]
    conv_rows(range(8), planes, two_ref[...], out_ref, held, out, sems, finish)


def call_second_layer(two, bias, first, token):
    return kernel_call(
        second_layer,
        "second_layer",
        [VM, VM, VM, VM],
        FIELD,
        HELD,
        4.2,
        HBM,
    )(two, bias, first, token)


def partner(value, axis, bit):
    count = lax.axis_size(axis)
    return lax.ppermute(value, axis, [(i, i ^ bit) for i in range(count)])


def four(value, even, odd, given=None):
    count = lax.axis_size("dp") * lax.axis_size("space")
    size = value.shape[0]
    even, odd = [(first, second, first ^ second) for first, second in (even, odd)]
    one, two, three = [
        lax.ppermute(
            given if n == 2 and given is not None else value,
            ("dp", "space"),
            [(i, i ^ (odd if i % 2 else even)[n]) for i in range(count)],
        )
        for n in range(3)
    ]
    total = (value + one) + (two + three[:size])
    return total if given is None else (total, three[size:])


def after(*values):
    return lax.optimization_barrier(values)


def local(activation, cotangent, volume, dec_weight, enc_grad, params, moment, second):
    act, cot, vol = activation[0], cotangent[0], volume[0, 0]
    count = lax.axis_size("space")
    devices = lax.axis_size("dp") * count
    voxels = devices * act.shape[1] * act.shape[2] * act.shape[3]
    scales = (1.0 / math.sqrt(voxels), 1.0 / math.sqrt(devices))
    table = jnp.asarray(placement())

    far, near = call_edges(cot, vol)
    pairs = [(i, i + 1) for i in range(1, count - 1, 2)]
    far_in = lax.ppermute(far, "space", pairs + [(b, a) for a, b in pairs])
    near_in = partner(near, "space", 1)

    far, enc_grad, act, cot = after(far, enc_grad, act, cot)
    enc = jnp.pad(enc_grad, ((0, 0), (0, 0), (0, 8192 - 7376))).reshape(64, 128)
    pad = lambda value: jnp.pad(value, (0, 2048 - 1786)).reshape(16, 128)
    own = jnp.concatenate([pad(params), pad(moment), pad(second)], axis=0)
    state = own

    def state_round(enc, state, bit):
        return partner(jnp.concatenate([enc, state], axis=0), "dp", bit)

    def joined(enc, state, got):
        return enc + got[:64], jnp.concatenate([state, got[64:]], axis=0)

    got = state_round(enc, state, 4)
    inner_grad, cot_rows, act_edge = call_inner(act, cot, enc)
    got, inner_grad = after(got, inner_grad)
    enc, state = joined(enc, state, got)
    got = state_round(enc, state, 2)
    kernel = call_turn_weights(dec_weight.transpose(1, 2, 0), enc)
    act_edge, kernel = after(act_edge, kernel)
    dec, rim_rows = call_outer(far_in, near_in, act_edge, inner_grad, enc)
    got, dec = after(got, dec)
    both, sent, state = call_merge(dec, enc, got, state)
    token = both
    along_y, along_x = (8, 8 + count), (4, 6)
    both, other = four(both, along_y, along_x, sent)
    grad_input = call_input_grad(0, kernel, cot_rows, rim_rows, token)
    both, grad_input = after(both, grad_input)
    token = both
    both = four(both, along_x, along_y)
    grad_input = call_input_grad(1, kernel, cot_rows, rim_rows, token, grad_input)
    both, grad_input = after(both, grad_input)
    token = both
    got = partner(jnp.concatenate([both, other], axis=0), "space", 1)
    cells = call_volume_windows(far_in, near_in, vol, token)
    got, cells = after(got, cells)
    both, state = call_gather_state(both, got, state, other)

    dec = both[:56]
    token = dec
    dec = dec + partner(dec, "dp", 2)
    two, one, bias = call_update_encoder(scales[1], both, state, table)
    first = call_first_layer(one, cells, token)
    dec, first = after(dec, first)
    token = dec
    dec = dec + partner(dec, "dp", 4)
    encoded = call_second_layer(two, bias, first, token)
    dec, encoded = after(dec, encoded)
    working, *new = call_finish(scales, dec, both, state, own)
    working = working.reshape(112 * 128)[:14288]
    return (grad_input[None], *new, working, encoded[None])


def solution(mesh):
    in_specs = (
        P("dp", None, "space", None, None),
        P("dp", None, "space", None, None),
        P("dp", None, "space", None, None),
        P(),
        P("dp", "space", None),
        P("dp"),
        P("dp"),
        P("dp"),
    )
    out_specs = (
        P("dp", None, "space", None, None),
        P("dp"),
        P("dp"),
        P("dp"),
        P(),
        P("dp", None, "space", None, None),
    )
    return jax.shard_map(local, mesh=mesh, in_specs=in_specs, out_specs=out_specs, check_vma=False)
```

```python
import functools
import math

import jax
import jax.numpy as jnp
import numpy as np
from jax import lax
from jax.experimental import pallas as pl
from jax.experimental.pallas import tpu as pltpu
from jax.sharding import PartitionSpec as P

BF = jnp.bfloat16
F32 = jnp.float32
LIMIT = 32 * 1024 * 1024


def exchange_matrix():
    rows = lax.broadcasted_iota(jnp.int32, (256, 256), 0)
    cols = lax.broadcasted_iota(jnp.int32, (256, 256), 1)
    return jnp.where(cols == (rows % 16) * 16 + rows // 16, 1.0, 0.0).astype(BF)


def mm(left, right):
    return lax.dot_general(left, right, (((1,), (0,)), ((), ())), preferred_element_type=F32)


def mm_lanes(left, right):
    return lax.dot_general(left, right, (((1,), (1,)), ((), ())), preferred_element_type=F32)


def lane_masks(rows):
    lanes = lax.broadcasted_iota(jnp.int32, (rows, 128), 1)
    return lanes != 0, lanes != 127


def from_left(value, keep):
    return jnp.where(keep, pltpu.roll(value, 1, 1), 0.0)


def from_right(value, keep):
    return jnp.where(keep, pltpu.roll(value, 127, 1), 0.0)


VM = pl.BlockSpec(memory_space=pltpu.VMEM)
HBM = pl.BlockSpec(memory_space=pltpu.HBM)


def kernel_call(
    body, name, in_specs, out_shape, scratch=(), micros=1.0, out_specs=None, aliases=None
):
    if out_specs is None:
        out_specs = jax.tree.map(lambda shape: VM, out_shape)
    return pl.pallas_call(
        body,
        in_specs=in_specs,
        out_specs=out_specs,
        out_shape=out_shape,
        input_output_aliases=aliases or {},
        scratch_shapes=list(scratch),
        compiler_params=pltpu.CompilerParams(vmem_limit_bytes=LIMIT),
        cost_estimate=pl.CostEstimate(
            flops=int(micros * 1.15e9), bytes_accessed=int(micros * 3.6e6), transcendentals=0
        ),
        name=name,
    )


def in_hbm(value):
    return pltpu.with_memory_space_constraint(value, pltpu.HBM)


def odd_place():
    return lax.rem(lax.axis_index("space"), 2)


def far_edge(cot_ref, vol_ref, far_ref, plane, slab, sems):
    side = odd_place()
    copies = [
        pltpu.make_async_copy(
            cot_ref.at[:, 3 * side, 32 * n : 32 * n + 32],
            plane.at[:, 32 * n : 32 * n + 32],
            sems.at[n],
        )
        for n in range(4)
    ]
    copies.append(pltpu.make_async_copy(vol_ref.at[pl.ds(2 * side, 2)], slab, sems.at[4]))
    for copy in copies:
        copy.start()
    for n in range(4):
        copies[n].wait()
        for j in (2 * n, 2 * n + 1):
            rows = slice(j * 16, (j + 1) * 16)
            far_ref[rows] = jnp.swapaxes(plane[:, rows], 0, 1)
    copies[4].wait()
    far_ref[128:144] = slab[...].reshape(16, 16, 128)


EDGE = jax.ShapeDtypeStruct((144, 16, 128), BF)


def call_far_edge(cot, vol):
    return kernel_call(
        far_edge,
        "far_edge",
        [HBM, HBM],
        EDGE,
        [
            pltpu.VMEM((16, 128, 128), BF),
            pltpu.VMEM((2, 128, 128), BF),
            pltpu.SemaphoreType.DMA((5,)),
        ],
        1.2,
    )(in_hbm(cot), in_hbm(vol))


def lateral(cells):
    zero = jnp.zeros((cells.shape[0], 1), BF)
    left = jnp.concatenate([zero, cells[:, :127]], axis=1)
    right = jnp.concatenate([cells[:, 1:], zero], axis=1)
    return left, cells, right


def aligned(total, rows, keep):
    out = []
    lanes = lax.broadcasted_iota(jnp.int32, (16, 256), 1) // 64
    for dx in range(3):
        summed = None
        for z, (turn, valid) in enumerate(keep):
            for r in range(2):
                start = ((dx * rows + z) * 2 + r) * 16
                part = total[start : start + 16]
                shift = (turn - r * 16) % 256
                if shift:
                    part = pltpu.roll(part, shift, 1)
                if valid is not None:
                    part = jnp.where((lanes >= valid[0]) & (lanes <= valid[1]), part, 0.0)
                summed = part if summed is None else summed + part
        out.append(summed)
    return jnp.concatenate(out, axis=0)


def inner(
    act_ref, cot_ref, vol_ref, token_ref, grad_ref, cot_rows, act_edge, near_ref, act_rows, total
):
    edge = jnp.zeros((4, 1, 16, 128), BF)
    cot_rows[:, 0:1] = edge
    cot_rows[:, 129:130] = edge
    total[...] = jnp.zeros_like(total)

    def turn(step):
        rows = pl.ds(step * 16, 16)
        for z in range(4):
            cot_rows[z, pl.ds(step * 16 + 1, 16)] = jnp.swapaxes(cot_ref[:, z, rows], 0, 1)
            cells = jnp.swapaxes(act_ref[:, z, rows], 0, 1).reshape(256, 128)
            for dx, value in enumerate(lateral(cells)):
                act_rows[dx, z, pl.ds(step * 16, 16)] = value.reshape(16, 16, 128)

    def gather(step):
        left, right = [], []
        for q in range(8):
            base = step * 16 + 2 * q
            left.append(
                jnp.concatenate(
                    [
                        act_rows[dx, z, pl.ds(base, 2)].reshape(32, 128)
                        for dx in range(3)
                        for z in range(4)
                    ],
                    axis=0,
                )
            )
            right.append(window([(cot_rows, z) for z in range(4)], base))
        total[...] += mm_lanes(jnp.concatenate(left, axis=1), jnp.concatenate(right, axis=1))

    turn(0)
    turn(1)

    for step in range(6):
        turn(step + 2)
        gather(step)
    gather(6)
    gather(7)
    grad_ref[...] = aligned(
        total, 4, [(64, (1, 2)), (0, None), (192, None), (128, (0, 1))]
    )
    side = 1 - odd_place()
    near_ref[0:128] = cot_rows[3 * side, 1:129]
    near_ref[128:144] = vol_ref[pl.ds(2 * side, 2)].reshape(16, 16, 128)
    act_edge[0] = act_rows[:, 0]
    act_edge[1] = act_rows[:, 3]


def call_inner(act, cot, vol, token):
    return kernel_call(
        inner,
        "inner",
        [VM, VM, VM, VM],
        [
            jax.ShapeDtypeStruct((48, 256), F32),
            jax.ShapeDtypeStruct((4, 130, 16, 128), BF),
            jax.ShapeDtypeStruct((2, 3, 128, 16, 128), BF),
            EDGE,
        ],
        [
            pltpu.VMEM((3, 4, 128, 16, 128), BF),
            pltpu.VMEM((384, 256), F32),
        ],
        4.0,
    )(act, cot, vol, token)


def window(planes, base):
    return jnp.concatenate(
        [ref[z, pl.ds(base, 4)].reshape(64, 128) for ref, z in planes], axis=0
    )


def flatten(summed, out_ref):
    lanes = lax.broadcasted_iota(jnp.int32, (8, 128), 1) // 16
    rows = lax.broadcasted_iota(jnp.int32, (8, 128), 0)
    out_ref[48:56] = jnp.zeros((8, 128), F32)
    for dx in range(3):
        for high in range(2):
            for half in range(2):
                start = dx * 16 + high * 8
                value = summed[start : start + 8, half * 128 : (half + 1) * 128]
                for bit in (1, 2, 4):
                    row_on, lane_on = (rows & bit) != 0, (lanes & bit) != 0
                    down = pltpu.roll(pltpu.roll(value, bit, 0), 128 - 16 * bit, 1)
                    up = pltpu.roll(pltpu.roll(value, 8 - bit, 0), 16 * bit, 1)
                    moved = jnp.where(row_on, down, up)
                    value = jnp.where(row_on == lane_on, value, moved)
                for place in range(8):
                    dz, dy = 2 - (half * 2 + place // 4), 2 - place % 4
                    if dz >= 0 and dy >= 0:
                        row = 2 * (9 * dz + 3 * dy + dx) + high
                        out_ref[row : row + 1] = value[place : place + 1]


def border_sum(side, rows, act_edge, total):
    total[...] = jnp.zeros_like(total)
    for step in range(2):
        left, right = [], []
        for q in range(32):
            base = step * 64 + 2 * q
            left.append(
                jnp.concatenate(
                    [act_edge[side, dx, base : base + 2].reshape(32, 128) for dx in range(3)],
                    axis=0,
                )
            )
            right.append(rows[base : base + 4].reshape(64, 128))
        total[:, 0:64] += mm_lanes(jnp.concatenate(left, axis=1), jnp.concatenate(right, axis=1))
    return pltpu.roll(aligned(total, 1, [(0, (0, 0))]), 128 * side, 1)


def outer_near(near_ref, act_edge, inner_ref, token_ref, grad_ref, rows_ref, total):
    edge = jnp.zeros((1, 16, 128), BF)
    rows_ref[0:1] = edge
    rows_ref[129:130] = edge
    rows_ref[1:129] = near_ref[0:128]
    grad_ref[...] = inner_ref[...] + border_sum(1 - odd_place(), rows_ref, act_edge, total)


def call_outer_near(near, act_edge, inner_grad, token):
    return kernel_call(
        outer_near,
        "outer_near",
        [VM, VM, VM, VM],
        [jax.ShapeDtypeStruct((48, 256), F32), jax.ShapeDtypeStruct((130, 16, 128), BF)],
        [pltpu.VMEM((96, 256), F32)],
        0.9,
    )(near, act_edge, inner_grad, token)


def outer_far(far_ref, act_edge, before_ref, near_rows, grad_ref, rim_ref, total):
    odd = odd_place()
    edge = jnp.zeros((1, 16, 128), BF)
    rows = rim_ref.at[odd]
    rows[0:1] = edge
    rows[129:130] = edge
    rows[1:129] = far_ref[0:128]
    flatten(before_ref[...] + border_sum(odd, rows, act_edge, total), grad_ref)
    rim_ref[1 - odd] = near_rows[...]


def call_outer_far(far, act_edge, before, near_rows):
    return kernel_call(
        outer_far,
        "outer_far",
        [VM, VM, VM, VM],
        [
            jax.ShapeDtypeStruct((56, 128), F32),
            jax.ShapeDtypeStruct((2, 130, 16, 128), BF),
        ],
        [pltpu.VMEM((96, 256), F32)],
        1.0,
    )(far, act_edge, before, near_rows)


def conv_rows(blocks, planes, kernel, out_hbm, held, out, sems, finish):
    swap = exchange_matrix()
    not_first, not_last = lane_masks(64)

    def compute(block):
        for q in range(8):
            base = block * 16 + 2 * q
            cells = jnp.concatenate(
                [window(planes[2 * zt : 2 * zt + 4], base) for zt in range(2)], axis=1
            )
            product = mm(kernel, cells)
            for zt in range(2):
                piece = product[:, zt * 128 : (zt + 1) * 128]
                summed = (
                    piece[64:128]
                    + from_left(piece[0:64], not_first)
                    + from_right(piece[128:192], not_last)
                )
                rounded = finish(summed).astype(BF).reshape(2, 2, 16, 128)
                for z in range(2):
                    held[block % 4, 2 * zt + z, 2 * q : 2 * q + 2] = rounded[z]

    def flush(block):
        rows = slice(block * 16, block * 16 + 16)
        for zt in range(2):
            cells = jnp.concatenate(
                [held[block % 4, 2 * zt + z].reshape(256, 128) for z in range(2)], axis=1
            )
            moved = mm(swap, cells).astype(BF)
            for z in range(2):
                piece = moved[:, z * 128 : (z + 1) * 128]
                out[:, 2 * zt + z, rows] = piece.reshape(16, 16, 128)
        copy = pltpu.make_async_copy(out.at[:, :, rows], out_hbm.at[:, :, rows], sems.at[block])
        copy.start()
        return copy

    copies = []
    for place, block in enumerate(blocks):
        compute(block)
        if place % 2 and place > 1:
            copies += [flush(blocks[place - 3]), flush(blocks[place - 2])]
    copies += [flush(block) for block in blocks[-2:]]
    for copy in copies:
        copy.wait()


FIELD = jax.ShapeDtypeStruct((16, 4, 128, 128), BF)
HELD = [
    pltpu.VMEM((4, 4, 16, 16, 128), BF),
    pltpu.VMEM((16, 4, 128, 128), BF),
    pltpu.SemaphoreType.DMA((8,)),
]


def shifted_kernels(bases):
    return jnp.concatenate(
        [
            pltpu.roll(base, (z * 4 + r) * 16, 1) if z + r else base
            for base in bases
            for z in range(2)
            for r in range(2)
        ],
        axis=0,
    ).astype(BF)


def input_grad(part, kernel_ref, cot_ref, rim_ref, token_ref, *refs):
    out_ref, held, out, sems = refs[-4:]
    planes = [(rim_ref, 0)] + [(cot_ref, z) for z in range(4)] + [(rim_ref, 1)]
    blocks = range(4 * part, 4 * part + 4)
    conv_rows(blocks, planes, kernel_ref[...], out_ref, held, out, sems, lambda value: value)


def call_input_grad(part, kernel, cot_rows, rim_rows, token, *before):
    return kernel_call(
        functools.partial(input_grad, part),
        f"input_grad_{part}",
        [VM, VM, VM, VM] + [HBM] * len(before),
        FIELD,
        HELD,
        2.2,
        HBM,
        {4: 0} if before else None,
    )(kernel, cot_rows, rim_rows, token, *before)


def placement():
    table = np.zeros((8, 64, 1408), np.float32)

    def put(group, column):
        table[group % 8, group // 8, column] = 1.0

    for dz in range(3):
        for dy in range(3):
            for dx in range(3):
                k = 9 * dz + 3 * dy + dx
                for i in range(16):
                    put(28 + k * 16 + i, dx * 256 + (dz * 4 + dy) * 16 + i)
                put(k, 896 + dx * 64 + dz * 16 + 3 + dy)
    for lane in range(128):
        put(28 + 27 * 16, 768 + lane)
    put(27, 1152 + 192)
    return table.astype(BF)


def adam(params, moment, second, gradient):
    new_moment = 0.9 * moment + 0.1 * gradient
    new_second = 0.999 * second + 0.001 * gradient * gradient
    new_params = params - 0.01 * new_moment / (jnp.sqrt(new_second) + 1e-08)
    return new_params, new_moment, new_second


def update_encoder(scale, grad_ref, state_ref, table_ref, two_ref, one_ref, bias_ref):
    gradient = grad_ref[54:112] * scale
    new = adam(state_ref[0, 54:112], state_ref[1, 54:112], state_ref[2, 54:112], gradient)[0]
    rows = lax.broadcasted_iota(jnp.int32, (58, 128), 0)
    lanes = lax.broadcasted_iota(jnp.int32, (58, 128), 1)
    clean = jnp.where(rows * 128 + lanes < 7376, new, 0.0)
    clean = jnp.concatenate([clean, jnp.zeros((6, 128), F32)], axis=0)
    turned = jnp.transpose(clean).astype(BF)
    groups = [turned[group * 16 : (group + 1) * 16] for group in range(8)]
    found = mm(jnp.concatenate(groups, axis=1), table_ref[...].reshape(512, 1408))
    two_ref[...] = shifted_kernels([found[:, dx * 256 : (dx + 1) * 256] for dx in range(3)])
    bias_ref[...] = found[:, 768:896]
    base, bias = found[:, 896:1152], found[:, 1152:1408]
    one_ref[...] = jnp.concatenate(
        [
            (pltpu.roll(base, z * 16 + r, 1) if z + r else base) + bias
            for z in range(2)
            for r in range(8)
        ],
        axis=0,
    ).astype(BF)


def call_update_encoder(scale, grad, state, table):
    return kernel_call(
        functools.partial(update_encoder, scale),
        "update_encoder",
        [VM, VM, VM],
        [
            jax.ShapeDtypeStruct((192, 256), BF),
            jax.ShapeDtypeStruct((256, 256), BF),
            jax.ShapeDtypeStruct((16, 128), F32),
        ],
        micros=0.6,
    )(grad, state, table)


def gather_state(both_ref, got_ref, half_ref, other_ref, sum_ref, out_ref):
    sum_ref[...] = both_ref[...] + got_ref[0:112]
    data = lax.axis_index("dp")
    odd = odd_place()
    lanes = lax.broadcasted_iota(jnp.int32, (16, 128), 1)
    for shard in range(8):
        away = lax.bitwise_xor(data, shard)
        slot = lax.bitwise_and(away, 2) + away // 4
        start = pl.multiple_of(48 * slot, 48)
        kept = 128 - 6 * shard
        for n in range(3):
            span = pl.ds(start + 16 * n, 16)
            there = pl.ds(start + 112 + 16 * n, 16)
            rows = jnp.where(odd == 1, got_ref[there], other_ref[span])
            rows = jnp.where(lax.rem(away, 2) == 1, rows, half_ref[span])
            if shard:
                rows = pltpu.roll(rows, kept, 1)
                before = out_ref[n, 14 * shard - 1 : 14 * shard]
                out_ref[n, 14 * shard - 1 : 14 * shard] = jnp.where(
                    lanes[:1] < kept, before, rows[:1]
                )
            out_ref[n, 14 * shard : 14 * shard + 14] = jnp.where(
                lanes[:14] < kept, rows[:14], rows[1:15]
            )


def call_gather_state(both, got, half, other):
    return kernel_call(
        gather_state,
        "gather_state",
        [VM, VM, VM, VM],
        [jax.ShapeDtypeStruct((112, 128), F32), jax.ShapeDtypeStruct((3, 112, 128), F32)],
        micros=0.3,
    )(both, got, half, other)


def merge(dec_ref, enc_ref, got_ref, state_ref, both_ref, sent_ref, all_ref):
    both_ref[0:54] = dec_ref[0:54]
    both_ref[54:112] = enc_ref[0:58] + got_ref[0:58]
    sent_ref[0:112] = both_ref[...]
    for out, first in ((sent_ref, 112), (all_ref, 0)):
        out[first : first + 96] = state_ref[...]
        out[first + 96 : first + 192] = got_ref[64:160]


def call_merge(dec, enc, got, state):
    return kernel_call(
        merge,
        "merge",
        [VM, VM, VM, VM],
        [jax.ShapeDtypeStruct((rows, 128), F32) for rows in (112, 304, 192)],
        micros=0.2,
    )(dec, enc, got, state)


def finish(scales, dec_ref, enc_ref, state_ref, own_ref, *refs):
    work_ref, *own_refs, flat = refs
    rows = lax.broadcasted_iota(jnp.int32, (112, 128), 0)
    gradient = enc_ref[...] * scales[1]
    dec = jnp.concatenate([dec_ref[...], jnp.zeros((56, 128), F32)], axis=0) * scales[0]
    gradient = jnp.where(rows < 54, dec, gradient)
    work_ref[...] = adam(state_ref[0], state_ref[1], state_ref[2], gradient)[0].astype(BF)
    flat[0:8] = jnp.zeros((8, 128), F32)
    flat[8:120] = gradient
    data = lax.axis_index("dp")
    turned = pltpu.roll(flat[pl.ds(7 + 14 * data, 15)], 6 * data, 1)
    lanes = lax.broadcasted_iota(jnp.int32, (14, 128), 1)
    own = jnp.where(lanes >= 6 * data, turned[1:15], turned[0:14])
    new = adam(own_ref[0:14], own_ref[16:30], own_ref[32:46], own)
    for value, out in zip(new, own_refs):
        for row in range(14):
            width = min(128, 1786 - 128 * row)
            out[pl.ds(128 * row, width)] = value[row][:width]


def call_finish(scales, dec, enc, state, own):
    shard = jax.ShapeDtypeStruct((1786,), F32)
    return kernel_call(
        functools.partial(finish, scales),
        "finish",
        [VM, VM, VM, VM],
        [jax.ShapeDtypeStruct((112, 128), BF), shard, shard, shard],
        [pltpu.VMEM((120, 128), F32)],
    )(dec, enc, state, own)


def volume_windows(far_ref, near_ref, volume_ref, token_ref, out_ref):
    not_first, not_last = lane_masks(128)
    odd = odd_place()
    for plane in range(8):
        if plane < 2 or plane > 5:
            z = plane if plane < 2 else plane - 6
            far, near = [
                ref[start : start + 8].reshape(128, 128).astype(F32)
                for ref, start in ((far_ref, 128 + 8 * z), (near_ref, 128 + 8 * z))
            ]
            cells = jnp.where(odd == (0 if plane < 2 else 1), far, near)
        else:
            cells = volume_ref[plane - 2]
        cells = cells.astype(F32)
        sides = (from_left(cells, not_first), cells, from_right(cells, not_last))
        pad = jnp.zeros((4, 128), F32)
        for dx in range(3):
            value = sides[dx]
            down = jnp.concatenate([pad, value[:124]], axis=0)
            up = jnp.concatenate([value[4:], pad], axis=0)
            out_ref[0, dx, plane] = down.astype(BF).reshape(8, 16, 128)
            out_ref[1, dx, plane] = up.astype(BF).reshape(8, 16, 128)


def call_volume_windows(far, near, volume, token):
    return kernel_call(
        volume_windows,
        "volume_windows",
        [VM, VM, VM, VM],
        jax.ShapeDtypeStruct((2, 3, 8, 8, 16, 128), BF),
        micros=0.5,
    )(far, near, volume, token)


def turn_weights(weight_ref, token_ref, kernel_ref):
    weight = weight_ref[...].reshape(256, 27)
    weight = jnp.concatenate([weight, jnp.zeros((256, 101), BF)], axis=1)
    taps = lax.broadcasted_iota(jnp.int32, (128, 768), 0)
    columns = lax.broadcasted_iota(jnp.int32, (128, 768), 1)
    dx, dz, dy = columns // 256, columns % 256 // 64, columns // 16 % 4
    wanted = (dz < 3) & (dy < 3) & (taps == 26 - (9 * dz + 3 * dy + dx))
    spread = mm(weight, jnp.where(wanted, 1.0, 0.0).astype(BF))
    rows = lax.broadcasted_iota(jnp.int32, (256, 768), 0)
    lanes = lax.broadcasted_iota(jnp.int32, (256, 768), 1)
    spread = jnp.where(rows % 16 == lanes % 16, spread, 0.0).astype(BF)
    places = lax.broadcasted_iota(jnp.int32, (16, 256), 0)
    inputs = lax.broadcasted_iota(jnp.int32, (16, 256), 1)
    found = mm(jnp.where(places == inputs // 16, 1.0, 0.0).astype(BF), spread)
    bases = [found[:, dx * 256 : (dx + 1) * 256] for dx in range(3)]
    kernel_ref[...] = shifted_kernels(bases)


def call_turn_weights(weight, token):
    return kernel_call(
        turn_weights,
        "turn_weights",
        [VM, VM],
        jax.ShapeDtypeStruct((192, 256), BF),
        micros=0.5,
    )(weight, token)


def first_layer(one_ref, cells_ref, token_ref, first):
    space = lax.axis_index("space")
    edge = jnp.zeros((6, 1, 16, 128), BF)
    first[:, 0:1] = edge
    first[:, 129:130] = edge
    rows = lax.broadcasted_iota(jnp.int32, (64, 256), 0)
    ones = jnp.where(rows == 0, 1.0, 0.0).astype(BF)
    kernel = one_ref[...]

    def body(half, carry):
        for part in range(4):
            j = half * 4 + part
            for zp in range(3):
                cells = jnp.concatenate(
                    [
                        jnp.concatenate(
                            [cells_ref[s, dx, 2 * zp + z, j] for s in range(2)], axis=1
                        )
                        for dx in range(3)
                        for z in range(4)
                    ]
                    + [ones],
                    axis=0,
                )
                product = jnp.maximum(mm(kernel, cells), 0.0)
                for s in range(2):
                    found = product[:, s * 128 : (s + 1) * 128].reshape(2, 128, 128)
                    for z in range(2):
                        plane = 2 * zp + z
                        value = found[z]
                        if plane == 0:
                            value = jnp.where(space > 0, value, 0.0)
                        if plane == 5:
                            value = jnp.where(space < lax.axis_size("space") - 1, value, 0.0)
                        value = value.astype(BF).reshape(8, 16, 128)
                        first[plane, pl.ds(j * 16 + s * 8 + 1, 8)] = value
        return carry

    lax.fori_loop(0, 2, body, 0)


def call_first_layer(one, cells, token):
    return kernel_call(
        first_layer,
        "first_layer",
        [VM, VM, VM],
        jax.ShapeDtypeStruct((6, 130, 16, 128), BF),
        micros=1.5,
    )(one, cells, token)


def second_layer(two_ref, bias_ref, first, token_ref, out_ref, held, out, sems):
    bias = jnp.concatenate([bias_ref[...]] * 4, axis=0)
    finish = lambda value: jnp.maximum(value + bias, 0.0)
    planes = [(first, z) for z in range(6)]
    conv_rows(range(8), planes, two_ref[...], out_ref, held, out, sems, finish)


def call_second_layer(two, bias, first, token):
    return kernel_call(
        second_layer,
        "second_layer",
        [VM, VM, VM, VM],
        FIELD,
        HELD,
        4.2,
        HBM,
    )(two, bias, first, token)


def partner(value, axis, bit):
    count = lax.axis_size(axis)
    return lax.ppermute(value, axis, [(i, i ^ bit) for i in range(count)])


def four(value, even, odd, given=None):
    count = lax.axis_size("dp") * lax.axis_size("space")
    size = value.shape[0]
    even, odd = [(first, second, first ^ second) for first, second in (even, odd)]
    one, two, three = [
        lax.ppermute(
            given if n == 2 and given is not None else value,
            ("dp", "space"),
            [(i, i ^ (odd if i % 2 else even)[n]) for i in range(count)],
        )
        for n in range(3)
    ]
    total = (value + one) + (two + three[:size])
    return total if given is None else (total, three[size:])


def after(*values):
    return lax.optimization_barrier(values)


def local(activation, cotangent, volume, dec_weight, enc_grad, params, moment, second):
    act, cot, vol = activation[0], cotangent[0], volume[0, 0]
    count = lax.axis_size("space")
    devices = lax.axis_size("dp") * count
    voxels = devices * act.shape[1] * act.shape[2] * act.shape[3]
    scales = (1.0 / math.sqrt(voxels), 1.0 / math.sqrt(devices))
    table = jnp.asarray(placement())

    far = call_far_edge(cot, vol)
    pairs = [(i, i + 1) for i in range(1, count - 1, 2)]
    far_in = lax.ppermute(far, "space", pairs + [(b, a) for a, b in pairs])

    far, enc_grad, act, cot = after(far, enc_grad, act, cot)
    enc = jnp.pad(enc_grad, ((0, 0), (0, 0), (0, 8192 - 7376))).reshape(64, 128)
    pad = lambda value: jnp.pad(value, (0, 2048 - 1786)).reshape(16, 128)
    own = jnp.concatenate([pad(params), pad(moment), pad(second)], axis=0)
    state = own

    def state_round(enc, state, bit):
        return partner(jnp.concatenate([enc, state], axis=0), "dp", bit)

    def joined(enc, state, got):
        return enc + got[:64], jnp.concatenate([state, got[64:]], axis=0)

    got = state_round(enc, state, 4)
    inner_grad, cot_rows, act_edge, near = call_inner(act, cot, vol, enc)
    near_in = partner(near, "space", 1)
    got, inner_grad = after(got, inner_grad)
    enc, state = joined(enc, state, got)
    got = state_round(enc, state, 2)
    kernel = call_turn_weights(dec_weight.transpose(1, 2, 0), enc)
    act_edge, kernel = after(act_edge, kernel)
    before, near_rows = call_outer_near(near_in, act_edge, inner_grad, enc)
    dec, rim_rows = call_outer_far(far_in, act_edge, before, near_rows)
    got, dec = after(got, dec)
    both, sent, state = call_merge(dec, enc, got, state)
    token = both
    along_y, along_x = (8, 8 + count), (4, 6)
    both, other = four(both, along_y, along_x, sent)
    grad_input = call_input_grad(0, kernel, cot_rows, rim_rows, token)
    both, grad_input = after(both, grad_input)
    token = both
    both = four(both, along_x, along_y)
    grad_input = call_input_grad(1, kernel, cot_rows, rim_rows, token, grad_input)
    both, grad_input = after(both, grad_input)
    token = both
    got = partner(jnp.concatenate([both, other], axis=0), "space", 1)
    cells = call_volume_windows(far_in, near_in, vol, token)
    got, cells = after(got, cells)
    both, state = call_gather_state(both, got, state, other)

    dec = both[:56]
    token = dec
    dec = dec + partner(dec, "dp", 2)
    two, one, bias = call_update_encoder(scales[1], both, state, table)
    first = call_first_layer(one, cells, token)
    dec, first = after(dec, first)
    token = dec
    dec = dec + partner(dec, "dp", 4)
    encoded = call_second_layer(two, bias, first, token)
    dec, encoded = after(dec, encoded)
    working, *new = call_finish(scales, dec, both, state, own)
    working = working.reshape(112 * 128)[:14288]
    return (grad_input[None], *new, working, encoded[None])


def solution(mesh):
    in_specs = (
        P("dp", None, "space", None, None),
        P("dp", None, "space", None, None),
        P("dp", None, "space", None, None),
        P(),
        P("dp", "space", None),
        P("dp"),
        P("dp"),
        P("dp"),
    )
    out_specs = (
        P("dp", None, "space", None, None),
        P("dp"),
        P("dp"),
        P("dp"),
        P(),
        P("dp", None, "space", None, None),
    )
    return jax.shard_map(local, mesh=mesh, in_specs=in_specs, out_specs=out_specs, check_vma=False)
```

```python
import functools
import math

import jax
import jax.numpy as jnp
import numpy as np
from jax import lax
from jax.experimental import pallas as pl
from jax.experimental.pallas import tpu as pltpu
from jax.sharding import PartitionSpec as P

BF = jnp.bfloat16
F32 = jnp.float32
LIMIT = 32 * 1024 * 1024


def exchange_matrix():
    rows = lax.broadcasted_iota(jnp.int32, (256, 256), 0)
    cols = lax.broadcasted_iota(jnp.int32, (256, 256), 1)
    return jnp.where(cols == (rows % 16) * 16 + rows // 16, 1.0, 0.0).astype(BF)


def mm(left, right):
    return lax.dot_general(left, right, (((1,), (0,)), ((), ())), preferred_element_type=F32)


def mm_lanes(left, right):
    return lax.dot_general(left, right, (((1,), (1,)), ((), ())), preferred_element_type=F32)


def lane_masks(rows):
    lanes = lax.broadcasted_iota(jnp.int32, (rows, 128), 1)
    return lanes != 0, lanes != 127


def from_left(value, keep):
    return jnp.where(keep, pltpu.roll(value, 1, 1), 0.0)


def from_right(value, keep):
    return jnp.where(keep, pltpu.roll(value, 127, 1), 0.0)


VM = pl.BlockSpec(memory_space=pltpu.VMEM)
HBM = pl.BlockSpec(memory_space=pltpu.HBM)


def kernel_call(
    body, name, in_specs, out_shape, scratch=(), micros=1.0, out_specs=None, aliases=None
):
    if out_specs is None:
        out_specs = jax.tree.map(lambda shape: VM, out_shape)
    return pl.pallas_call(
        body,
        in_specs=in_specs,
        out_specs=out_specs,
        out_shape=out_shape,
        input_output_aliases=aliases or {},
        scratch_shapes=list(scratch),
        compiler_params=pltpu.CompilerParams(vmem_limit_bytes=LIMIT),
        cost_estimate=pl.CostEstimate(
            flops=int(micros * 1.15e9), bytes_accessed=int(micros * 3.6e6), transcendentals=0
        ),
        name=name,
    )


def in_hbm(value):
    return pltpu.with_memory_space_constraint(value, pltpu.HBM)


def odd_place():
    return lax.rem(lax.axis_index("space"), 2)


def far_edge(cot_ref, vol_ref, far_ref, plane, slab, sems):
    side = odd_place()
    copies = [
        pltpu.make_async_copy(
            cot_ref.at[:, 3 * side, 32 * n : 32 * n + 32],
            plane.at[:, 32 * n : 32 * n + 32],
            sems.at[n],
        )
        for n in range(4)
    ]
    copies.append(pltpu.make_async_copy(vol_ref.at[pl.ds(2 * side, 2)], slab, sems.at[4]))
    for copy in copies:
        copy.start()
    for n in range(4):
        copies[n].wait()
        for j in (2 * n, 2 * n + 1):
            rows = slice(j * 16, (j + 1) * 16)
            far_ref[rows] = jnp.swapaxes(plane[:, rows], 0, 1)
    copies[4].wait()
    far_ref[128:144] = slab[...].reshape(16, 16, 128)


EDGE = jax.ShapeDtypeStruct((144, 16, 128), BF)


def call_far_edge(cot, vol):
    return kernel_call(
        far_edge,
        "far_edge",
        [HBM, HBM],
        EDGE,
        [
            pltpu.VMEM((16, 128, 128), BF),
            pltpu.VMEM((2, 128, 128), BF),
            pltpu.SemaphoreType.DMA((5,)),
        ],
        1.2,
    )(in_hbm(cot), in_hbm(vol))


def lateral(cells):
    zero = jnp.zeros((cells.shape[0], 1), BF)
    left = jnp.concatenate([zero, cells[:, :127]], axis=1)
    right = jnp.concatenate([cells[:, 1:], zero], axis=1)
    return left, cells, right


def aligned(total, rows, keep):
    out = []
    lanes = lax.broadcasted_iota(jnp.int32, (16, 256), 1) // 64
    for dx in range(3):
        summed = None
        for z, (turn, valid) in enumerate(keep):
            for r in range(2):
                start = ((dx * rows + z) * 2 + r) * 16
                part = total[start : start + 16]
                shift = (turn - r * 16) % 256
                if shift:
                    part = pltpu.roll(part, shift, 1)
                if valid is not None:
                    part = jnp.where((lanes >= valid[0]) & (lanes <= valid[1]), part, 0.0)
                summed = part if summed is None else summed + part
        out.append(summed)
    return jnp.concatenate(out, axis=0)


def inner(
    act_ref, cot_ref, vol_ref, token_ref, grad_ref, cot_rows, act_edge, near_ref, act_rows, total
):
    edge = jnp.zeros((4, 1, 16, 128), BF)
    cot_rows[:, 0:1] = edge
    cot_rows[:, 129:130] = edge
    total[...] = jnp.zeros_like(total)

    def turn(step):
        rows = pl.ds(step * 16, 16)
        for z in range(4):
            cot_rows[z, pl.ds(step * 16 + 1, 16)] = jnp.swapaxes(cot_ref[:, z, rows], 0, 1)
            cells = jnp.swapaxes(act_ref[:, z, rows], 0, 1).reshape(256, 128)
            for dx, value in enumerate(lateral(cells)):
                act_rows[dx, z, pl.ds(step * 16, 16)] = value.reshape(16, 16, 128)

    def gather(step):
        left, right = [], []
        for q in range(8):
            base = step * 16 + 2 * q
            left.append(
                jnp.concatenate(
                    [
                        act_rows[dx, z, pl.ds(base, 2)].reshape(32, 128)
                        for dx in range(3)
                        for z in range(4)
                    ],
                    axis=0,
                )
            )
            right.append(window([(cot_rows, z) for z in range(4)], base))
        total[...] += mm_lanes(jnp.concatenate(left, axis=1), jnp.concatenate(right, axis=1))

    turn(0)
    turn(1)

    for step in range(6):
        turn(step + 2)
        gather(step)
    gather(6)
    gather(7)
    grad_ref[...] = aligned(
        total, 4, [(64, (1, 2)), (0, None), (192, None), (128, (0, 1))]
    )
    side = 1 - odd_place()
    near_ref[0:128] = cot_rows[3 * side, 1:129]
    near_ref[128:144] = vol_ref[pl.ds(2 * side, 2)].reshape(16, 16, 128)
    act_edge[0] = act_rows[:, 0]
    act_edge[1] = act_rows[:, 3]


def call_inner(act, cot, vol, token):
    return kernel_call(
        inner,
        "inner",
        [VM, VM, VM, VM],
        [
            jax.ShapeDtypeStruct((48, 256), F32),
            jax.ShapeDtypeStruct((4, 130, 16, 128), BF),
            jax.ShapeDtypeStruct((2, 3, 128, 16, 128), BF),
            EDGE,
        ],
        [
            pltpu.VMEM((3, 4, 128, 16, 128), BF),
            pltpu.VMEM((384, 256), F32),
        ],
        4.0,
    )(act, cot, vol, token)


def window(planes, base):
    return jnp.concatenate(
        [ref[z, pl.ds(base, 4)].reshape(64, 128) for ref, z in planes], axis=0
    )


def flatten(summed, out_ref):
    lanes = lax.broadcasted_iota(jnp.int32, (8, 128), 1) // 16
    rows = lax.broadcasted_iota(jnp.int32, (8, 128), 0)
    out_ref[48:56] = jnp.zeros((8, 128), F32)
    for dx in range(3):
        for high in range(2):
            for half in range(2):
                start = dx * 16 + high * 8
                value = summed[start : start + 8, half * 128 : (half + 1) * 128]
                for bit in (1, 2, 4):
                    row_on, lane_on = (rows & bit) != 0, (lanes & bit) != 0
                    down = pltpu.roll(pltpu.roll(value, bit, 0), 128 - 16 * bit, 1)
                    up = pltpu.roll(pltpu.roll(value, 8 - bit, 0), 16 * bit, 1)
                    moved = jnp.where(row_on, down, up)
                    value = jnp.where(row_on == lane_on, value, moved)
                for place in range(8):
                    dz, dy = 2 - (half * 2 + place // 4), 2 - place % 4
                    if dz >= 0 and dy >= 0:
                        row = 2 * (9 * dz + 3 * dy + dx) + high
                        out_ref[row : row + 1] = value[place : place + 1]


def border_sum(side, rows, act_edge, total):
    total[...] = jnp.zeros_like(total)
    for step in range(2):
        left, right = [], []
        for q in range(32):
            base = step * 64 + 2 * q
            left.append(
                jnp.concatenate(
                    [act_edge[side, dx, base : base + 2].reshape(32, 128) for dx in range(3)],
                    axis=0,
                )
            )
            right.append(rows[base : base + 4].reshape(64, 128))
        total[:, 0:64] += mm_lanes(jnp.concatenate(left, axis=1), jnp.concatenate(right, axis=1))
    return pltpu.roll(aligned(total, 1, [(0, (0, 0))]), 128 * side, 1)


def outer_near(near_ref, act_edge, inner_ref, token_ref, grad_ref, rows_ref, total):
    edge = jnp.zeros((1, 16, 128), BF)
    rows_ref[0:1] = edge
    rows_ref[129:130] = edge
    rows_ref[1:129] = near_ref[0:128]
    grad_ref[...] = inner_ref[...] + border_sum(1 - odd_place(), rows_ref, act_edge, total)


def call_outer_near(near, act_edge, inner_grad, token):
    return kernel_call(
        outer_near,
        "outer_near",
        [VM, VM, VM, VM],
        [jax.ShapeDtypeStruct((48, 256), F32), jax.ShapeDtypeStruct((130, 16, 128), BF)],
        [pltpu.VMEM((96, 256), F32)],
        0.9,
    )(near, act_edge, inner_grad, token)


def outer_far(far_ref, act_edge, before_ref, near_rows, grad_ref, rim_ref, total):
    odd = odd_place()
    edge = jnp.zeros((1, 16, 128), BF)
    rows = rim_ref.at[odd]
    rows[0:1] = edge
    rows[129:130] = edge
    rows[1:129] = far_ref[0:128]
    flatten(before_ref[...] + border_sum(odd, rows, act_edge, total), grad_ref)
    rim_ref[1 - odd] = near_rows[...]


def call_outer_far(far, act_edge, before, near_rows):
    return kernel_call(
        outer_far,
        "outer_far",
        [VM, VM, VM, VM],
        [
            jax.ShapeDtypeStruct((56, 128), F32),
            jax.ShapeDtypeStruct((2, 130, 16, 128), BF),
        ],
        [pltpu.VMEM((96, 256), F32)],
        1.0,
    )(far, act_edge, before, near_rows)


def conv_rows(blocks, planes, kernel, out_hbm, held, out, sems, finish):
    swap = exchange_matrix()
    not_first, not_last = lane_masks(64)

    def compute(block):
        for q in range(8):
            base = block * 16 + 2 * q
            cells = jnp.concatenate(
                [window(planes[2 * zt : 2 * zt + 4], base) for zt in range(2)], axis=1
            )
            product = mm(kernel, cells)
            for zt in range(2):
                piece = product[:, zt * 128 : (zt + 1) * 128]
                summed = (
                    piece[64:128]
                    + from_left(piece[0:64], not_first)
                    + from_right(piece[128:192], not_last)
                )
                rounded = finish(summed).astype(BF).reshape(2, 2, 16, 128)
                for z in range(2):
                    held[block % 4, 2 * zt + z, 2 * q : 2 * q + 2] = rounded[z]

    def flush(block):
        rows = slice(block * 16, block * 16 + 16)
        for zt in range(2):
            cells = jnp.concatenate(
                [held[block % 4, 2 * zt + z].reshape(256, 128) for z in range(2)], axis=1
            )
            moved = mm(swap, cells).astype(BF)
            for z in range(2):
                piece = moved[:, z * 128 : (z + 1) * 128]
                out[:, 2 * zt + z, rows] = piece.reshape(16, 16, 128)
        copy = pltpu.make_async_copy(out.at[:, :, rows], out_hbm.at[:, :, rows], sems.at[block])
        copy.start()
        return copy

    copies = []
    for place, block in enumerate(blocks):
        compute(block)
        if place:
            copies.append(flush(blocks[place - 1]))
    copies.append(flush(blocks[-1]))
    for copy in copies:
        copy.wait()


FIELD = jax.ShapeDtypeStruct((16, 4, 128, 128), BF)
HELD = [
    pltpu.VMEM((4, 4, 16, 16, 128), BF),
    pltpu.VMEM((16, 4, 128, 128), BF),
    pltpu.SemaphoreType.DMA((8,)),
]


def shifted_kernels(bases):
    return jnp.concatenate(
        [
            pltpu.roll(base, (z * 4 + r) * 16, 1) if z + r else base
            for base in bases
            for z in range(2)
            for r in range(2)
        ],
        axis=0,
    ).astype(BF)


def input_grad(part, kernel_ref, cot_ref, rim_ref, token_ref, *refs):
    out_ref, held, out, sems = refs[-4:]
    planes = [(rim_ref, 0)] + [(cot_ref, z) for z in range(4)] + [(rim_ref, 1)]
    blocks = range(4 * part, 4 * part + 4)
    conv_rows(blocks, planes, kernel_ref[...], out_ref, held, out, sems, lambda value: value)


def call_input_grad(part, kernel, cot_rows, rim_rows, token, *before):
    return kernel_call(
        functools.partial(input_grad, part),
        f"input_grad_{part}",
        [VM, VM, VM, VM] + [HBM] * len(before),
        FIELD,
        HELD,
        2.2,
        HBM,
        {4: 0} if before else None,
    )(kernel, cot_rows, rim_rows, token, *before)


def placement():
    table = np.zeros((8, 64, 1408), np.float32)

    def put(group, column):
        table[group % 8, group // 8, column] = 1.0

    for dz in range(3):
        for dy in range(3):
            for dx in range(3):
                k = 9 * dz + 3 * dy + dx
                for i in range(16):
                    put(28 + k * 16 + i, dx * 256 + (dz * 4 + dy) * 16 + i)
                put(k, 896 + dx * 64 + dz * 16 + 3 + dy)
    for lane in range(128):
        put(28 + 27 * 16, 768 + lane)
    put(27, 1152 + 192)
    return table.astype(BF)


def adam(params, moment, second, gradient):
    new_moment = 0.9 * moment + 0.1 * gradient
    new_second = 0.999 * second + 0.001 * gradient * gradient
    new_params = params - 0.01 * new_moment / (jnp.sqrt(new_second) + 1e-08)
    return new_params, new_moment, new_second


def update_encoder(scale, grad_ref, state_ref, table_ref, two_ref, one_ref, bias_ref):
    gradient = grad_ref[54:112] * scale
    new = adam(state_ref[0, 54:112], state_ref[1, 54:112], state_ref[2, 54:112], gradient)[0]
    rows = lax.broadcasted_iota(jnp.int32, (58, 128), 0)
    lanes = lax.broadcasted_iota(jnp.int32, (58, 128), 1)
    clean = jnp.where(rows * 128 + lanes < 7376, new, 0.0)
    clean = jnp.concatenate([clean, jnp.zeros((6, 128), F32)], axis=0)
    turned = jnp.transpose(clean).astype(BF)
    groups = [turned[group * 16 : (group + 1) * 16] for group in range(8)]
    found = mm(jnp.concatenate(groups, axis=1), table_ref[...].reshape(512, 1408))
    two_ref[...] = shifted_kernels([found[:, dx * 256 : (dx + 1) * 256] for dx in range(3)])
    bias_ref[...] = found[:, 768:896]
    base, bias = found[:, 896:1152], found[:, 1152:1408]
    one_ref[...] = jnp.concatenate(
        [
            (pltpu.roll(base, z * 16 + r, 1) if z + r else base) + bias
            for z in range(2)
            for r in range(8)
        ],
        axis=0,
    ).astype(BF)


def call_update_encoder(scale, grad, state, table):
    return kernel_call(
        functools.partial(update_encoder, scale),
        "update_encoder",
        [VM, VM, VM],
        [
            jax.ShapeDtypeStruct((192, 256), BF),
            jax.ShapeDtypeStruct((256, 256), BF),
            jax.ShapeDtypeStruct((16, 128), F32),
        ],
        micros=0.6,
    )(grad, state, table)


def gather_state(both_ref, got_ref, half_ref, other_ref, sum_ref, out_ref):
    sum_ref[...] = both_ref[...] + got_ref[0:112]
    data = lax.axis_index("dp")
    odd = odd_place()
    lanes = lax.broadcasted_iota(jnp.int32, (16, 128), 1)
    for shard in range(8):
        away = lax.bitwise_xor(data, shard)
        slot = lax.bitwise_and(away, 2) + away // 4
        start = pl.multiple_of(48 * slot, 48)
        kept = 128 - 6 * shard
        for n in range(3):
            span = pl.ds(start + 16 * n, 16)
            there = pl.ds(start + 112 + 16 * n, 16)
            rows = jnp.where(odd == 1, got_ref[there], other_ref[span])
            rows = jnp.where(lax.rem(away, 2) == 1, rows, half_ref[span])
            if shard:
                rows = pltpu.roll(rows, kept, 1)
                before = out_ref[n, 14 * shard - 1 : 14 * shard]
                out_ref[n, 14 * shard - 1 : 14 * shard] = jnp.where(
                    lanes[:1] < kept, before, rows[:1]
                )
            out_ref[n, 14 * shard : 14 * shard + 14] = jnp.where(
                lanes[:14] < kept, rows[:14], rows[1:15]
            )


def call_gather_state(both, got, half, other):
    return kernel_call(
        gather_state,
        "gather_state",
        [VM, VM, VM, VM],
        [jax.ShapeDtypeStruct((112, 128), F32), jax.ShapeDtypeStruct((3, 112, 128), F32)],
        micros=0.3,
    )(both, got, half, other)


def merge(dec_ref, enc_ref, got_ref, state_ref, both_ref, sent_ref, all_ref):
    both_ref[0:54] = dec_ref[0:54]
    both_ref[54:112] = enc_ref[0:58] + got_ref[0:58]
    sent_ref[0:112] = both_ref[...]
    for out, first in ((sent_ref, 112), (all_ref, 0)):
        out[first : first + 96] = state_ref[...]
        out[first + 96 : first + 192] = got_ref[64:160]


def call_merge(dec, enc, got, state):
    return kernel_call(
        merge,
        "merge",
        [VM, VM, VM, VM],
        [jax.ShapeDtypeStruct((rows, 128), F32) for rows in (112, 304, 192)],
        micros=0.2,
    )(dec, enc, got, state)


def finish(scales, dec_ref, enc_ref, state_ref, own_ref, *refs):
    work_ref, *own_refs, flat = refs
    rows = lax.broadcasted_iota(jnp.int32, (112, 128), 0)
    gradient = enc_ref[...] * scales[1]
    dec = jnp.concatenate([dec_ref[...], jnp.zeros((56, 128), F32)], axis=0) * scales[0]
    gradient = jnp.where(rows < 54, dec, gradient)
    work_ref[...] = adam(state_ref[0], state_ref[1], state_ref[2], gradient)[0].astype(BF)
    flat[0:8] = jnp.zeros((8, 128), F32)
    flat[8:120] = gradient
    data = lax.axis_index("dp")
    turned = pltpu.roll(flat[pl.ds(7 + 14 * data, 15)], 6 * data, 1)
    lanes = lax.broadcasted_iota(jnp.int32, (14, 128), 1)
    own = jnp.where(lanes >= 6 * data, turned[1:15], turned[0:14])
    new = adam(own_ref[0:14], own_ref[16:30], own_ref[32:46], own)
    for value, out in zip(new, own_refs):
        for row in range(14):
            width = min(128, 1786 - 128 * row)
            out[pl.ds(128 * row, width)] = value[row][:width]


def call_finish(scales, dec, enc, state, own):
    shard = jax.ShapeDtypeStruct((1786,), F32)
    return kernel_call(
        functools.partial(finish, scales),
        "finish",
        [VM, VM, VM, VM],
        [jax.ShapeDtypeStruct((112, 128), BF), shard, shard, shard],
        [pltpu.VMEM((120, 128), F32)],
    )(dec, enc, state, own)


def volume_windows(far_ref, near_ref, volume_ref, token_ref, out_ref):
    not_first, not_last = lane_masks(128)
    odd = odd_place()
    for plane in range(8):
        if plane < 2 or plane > 5:
            z = plane if plane < 2 else plane - 6
            far, near = [
                ref[start : start + 8].reshape(128, 128).astype(F32)
                for ref, start in ((far_ref, 128 + 8 * z), (near_ref, 128 + 8 * z))
            ]
            cells = jnp.where(odd == (0 if plane < 2 else 1), far, near)
        else:
            cells = volume_ref[plane - 2]
        cells = cells.astype(F32)
        sides = (from_left(cells, not_first), cells, from_right(cells, not_last))
        pad = jnp.zeros((4, 128), F32)
        for dx in range(3):
            value = sides[dx]
            down = jnp.concatenate([pad, value[:124]], axis=0)
            up = jnp.concatenate([value[4:], pad], axis=0)
            out_ref[0, dx, plane] = down.astype(BF).reshape(8, 16, 128)
            out_ref[1, dx, plane] = up.astype(BF).reshape(8, 16, 128)


def call_volume_windows(far, near, volume, token):
    return kernel_call(
        volume_windows,
        "volume_windows",
        [VM, VM, VM, VM],
        jax.ShapeDtypeStruct((2, 3, 8, 8, 16, 128), BF),
        micros=0.5,
    )(far, near, volume, token)


def turn_weights(weight_ref, token_ref, kernel_ref):
    weight = weight_ref[...].reshape(256, 27)
    weight = jnp.concatenate([weight, jnp.zeros((256, 101), BF)], axis=1)
    taps = lax.broadcasted_iota(jnp.int32, (128, 768), 0)
    columns = lax.broadcasted_iota(jnp.int32, (128, 768), 1)
    dx, dz, dy = columns // 256, columns % 256 // 64, columns // 16 % 4
    wanted = (dz < 3) & (dy < 3) & (taps == 26 - (9 * dz + 3 * dy + dx))
    spread = mm(weight, jnp.where(wanted, 1.0, 0.0).astype(BF))
    rows = lax.broadcasted_iota(jnp.int32, (256, 768), 0)
    lanes = lax.broadcasted_iota(jnp.int32, (256, 768), 1)
    spread = jnp.where(rows % 16 == lanes % 16, spread, 0.0).astype(BF)
    places = lax.broadcasted_iota(jnp.int32, (16, 256), 0)
    inputs = lax.broadcasted_iota(jnp.int32, (16, 256), 1)
    found = mm(jnp.where(places == inputs // 16, 1.0, 0.0).astype(BF), spread)
    bases = [found[:, dx * 256 : (dx + 1) * 256] for dx in range(3)]
    kernel_ref[...] = shifted_kernels(bases)


def call_turn_weights(weight, token):
    return kernel_call(
        turn_weights,
        "turn_weights",
        [VM, VM],
        jax.ShapeDtypeStruct((192, 256), BF),
        micros=0.5,
    )(weight, token)


def first_layer(one_ref, cells_ref, token_ref, first):
    space = lax.axis_index("space")
    edge = jnp.zeros((6, 1, 16, 128), BF)
    first[:, 0:1] = edge
    first[:, 129:130] = edge
    rows = lax.broadcasted_iota(jnp.int32, (64, 256), 0)
    ones = jnp.where(rows == 0, 1.0, 0.0).astype(BF)
    kernel = one_ref[...]

    def body(half, carry):
        for part in range(4):
            j = half * 4 + part
            for zp in range(3):
                cells = jnp.concatenate(
                    [
                        jnp.concatenate(
                            [cells_ref[s, dx, 2 * zp + z, j] for s in range(2)], axis=1
                        )
                        for dx in range(3)
                        for z in range(4)
                    ]
                    + [ones],
                    axis=0,
                )
                product = jnp.maximum(mm(kernel, cells), 0.0)
                for s in range(2):
                    found = product[:, s * 128 : (s + 1) * 128].reshape(2, 128, 128)
                    for z in range(2):
                        plane = 2 * zp + z
                        value = found[z]
                        if plane == 0:
                            value = jnp.where(space > 0, value, 0.0)
                        if plane == 5:
                            value = jnp.where(space < lax.axis_size("space") - 1, value, 0.0)
                        value = value.astype(BF).reshape(8, 16, 128)
                        first[plane, pl.ds(j * 16 + s * 8 + 1, 8)] = value
        return carry

    lax.fori_loop(0, 2, body, 0)


def call_first_layer(one, cells, token):
    return kernel_call(
        first_layer,
        "first_layer",
        [VM, VM, VM],
        jax.ShapeDtypeStruct((6, 130, 16, 128), BF),
        micros=1.5,
    )(one, cells, token)


def second_layer(two_ref, bias_ref, first, token_ref, out_ref, held, out, sems):
    bias = jnp.concatenate([bias_ref[...]] * 4, axis=0)
    finish = lambda value: jnp.maximum(value + bias, 0.0)
    planes = [(first, z) for z in range(6)]
    conv_rows(range(8), planes, two_ref[...], out_ref, held, out, sems, finish)


def call_second_layer(two, bias, first, token):
    return kernel_call(
        second_layer,
        "second_layer",
        [VM, VM, VM, VM],
        FIELD,
        HELD,
        4.2,
        HBM,
    )(two, bias, first, token)


def partner(value, axis, bit):
    count = lax.axis_size(axis)
    return lax.ppermute(value, axis, [(i, i ^ bit) for i in range(count)])


def four(value, even, odd, given=None):
    count = lax.axis_size("dp") * lax.axis_size("space")
    size = value.shape[0]
    even, odd = [(first, second, first ^ second) for first, second in (even, odd)]
    one, two, three = [
        lax.ppermute(
            given if n == 2 and given is not None else value,
            ("dp", "space"),
            [(i, i ^ (odd if i % 2 else even)[n]) for i in range(count)],
        )
        for n in range(3)
    ]
    total = (value + one) + (two + three[:size])
    return total if given is None else (total, three[size:])


def after(*values):
    return lax.optimization_barrier(values)


def local(activation, cotangent, volume, dec_weight, enc_grad, params, moment, second):
    act, cot, vol = activation[0], cotangent[0], volume[0, 0]
    count = lax.axis_size("space")
    devices = lax.axis_size("dp") * count
    voxels = devices * act.shape[1] * act.shape[2] * act.shape[3]
    scales = (1.0 / math.sqrt(voxels), 1.0 / math.sqrt(devices))
    table = jnp.asarray(placement())

    far = call_far_edge(cot, vol)
    pairs = [(i, i + 1) for i in range(1, count - 1, 2)]
    far_in = lax.ppermute(far, "space", pairs + [(b, a) for a, b in pairs])

    far, enc_grad, act, cot, vol = after(far, enc_grad, act, cot, vol)
    enc = jnp.pad(enc_grad, ((0, 0), (0, 0), (0, 8192 - 7376))).reshape(64, 128)
    pad = lambda value: jnp.pad(value, (0, 2048 - 1786)).reshape(16, 128)
    own = jnp.concatenate([pad(params), pad(moment), pad(second)], axis=0)
    state = own

    def state_round(enc, state, bit):
        return partner(jnp.concatenate([enc, state], axis=0), "dp", bit)

    def joined(enc, state, got):
        return enc + got[:64], jnp.concatenate([state, got[64:]], axis=0)

    got = state_round(enc, state, 4)
    inner_grad, cot_rows, act_edge, near = call_inner(act, cot, vol, enc)
    near_in = partner(near, "space", 1)
    got, inner_grad = after(got, inner_grad)
    enc, state = joined(enc, state, got)
    got = state_round(enc, state, 2)
    kernel = call_turn_weights(dec_weight.transpose(1, 2, 0), enc)
    act_edge, kernel = after(act_edge, kernel)
    before, near_rows = call_outer_near(near_in, act_edge, inner_grad, enc)
    dec, rim_rows = call_outer_far(far_in, act_edge, before, near_rows)
    got, dec = after(got, dec)
    both, sent, state = call_merge(dec, enc, got, state)
    token = both
    along_y, along_x = (8, 8 + count), (4, 6)
    both, other = four(both, along_y, along_x, sent)
    grad_input = call_input_grad(0, kernel, cot_rows, rim_rows, token)
    both, grad_input = after(both, grad_input)
    token = both
    both = four(both, along_x, along_y)
    grad_input = call_input_grad(1, kernel, cot_rows, rim_rows, token, grad_input)
    both, grad_input = after(both, grad_input)
    token = both
    got = partner(jnp.concatenate([both, other], axis=0), "space", 1)
    cells = call_volume_windows(far_in, near_in, vol, token)
    got, cells = after(got, cells)
    both, state = call_gather_state(both, got, state, other)

    dec = both[:56]
    token = dec
    dec = dec + partner(dec, "dp", 2)
    two, one, bias = call_update_encoder(scales[1], both, state, table)
    first = call_first_layer(one, cells, token)
    dec, first = after(dec, first)
    token = dec
    dec = dec + partner(dec, "dp", 4)
    encoded = call_second_layer(two, bias, first, token)
    dec, encoded = after(dec, encoded)
    working, *new = call_finish(scales, dec, both, state, own)
    working = working.reshape(112 * 128)[:14288]
    return (grad_input[None], *new, working, encoded[None])


def solution(mesh):
    in_specs = (
        P("dp", None, "space", None, None),
        P("dp", None, "space", None, None),
        P("dp", None, "space", None, None),
        P(),
        P("dp", "space", None),
        P("dp"),
        P("dp"),
        P("dp"),
    )
    out_specs = (
        P("dp", None, "space", None, None),
        P("dp"),
        P("dp"),
        P("dp"),
        P(),
        P("dp", None, "space", None, None),
    )
    return jax.shard_map(local, mesh=mesh, in_specs=in_specs, out_specs=out_specs, check_vma=False)
```
